256 devices in a mesh: gx: 32 (over x, y, core), gy: 8 (over z).
Axes of the slice: x: 4, y: 4, z: 8, core: 2. Of those that a mesh axis runs over, the one named last changes fastest.
Arguments:
- velocity: float32 [3, 1024, 256, 128], P(None, 'gx', 'gy'), may hold values from -5 to 5
- point_cells: int32 [3, 32, 8, 256], P(None, 'gx', 'gy'), may hold values from 0 to 1023, as said below
- point_offsets: float32 [3, 32, 8, 256], P(None, 'gx', 'gy'), may hold values from 0 to 1
- point_count: int32 [32, 8], P('gx', 'gy'), may hold values from 32 to 256, as said below
- drag: float32 [32, 8, 256], P('gx', 'gy'), may hold values from 30 to 300
- blade_speed: float32 [32, 8, 256], P('gx', 'gy'), may hold values from 0.5 to 2
Outputs:
- new_velocity: float32 [3, 1024, 256, 128], P(None, 'gx', 'gy')
- pressure: float32 [1024, 256, 128], P('gx', 'gy')
The draws below stay inside these ranges and needn't reach their ends.
Inputs may be any that keep to these rules, and one draw needn't show every extreme that they name: Every point's cell lies in the grid block of the device that holds the point: point_cells[0, i, j, s] is in [i * 32, (i + 1) * 32), point_cells[1, i, j, s] in [j * 32, (j + 1) * 32), point_cells[2] in [0, 128). `point_count`: some device is full in every draw; loads are skewed.
All inputs are finite; a program needn't handle non-finite values.
Results may differ from the reference program's by a relative error of at most 0.0003.
Values sent between devices are 32-bit elements; how exact they have to be, the bound alone decides.
No kernel may reach another device: no remote copies, remote signals or barrier semaphores. Data moves between devices by JAX's collectives and lax.ppermute only.
A program may use at most 192 MiB of HBM per device.

```python
import math
import jax
import jax.numpy as jnp
from jax import lax

CX = 32
CY = 32
NZ = 128
PTS_TILE = 256
LEVELS = 6
PRE_SWEEPS = 2
POST_SWEEPS = 1
COARSE_SWEEPS = 4
CYCLES = 2
NX = 1024
NY = 256
N_GX = 32
N_GY = 8


def draw_velocity(key, part):
    key = jax.random.fold_in(key, 5)
    return jnp.clip(jax.random.normal(key, (3, NX, NY, NZ), jnp.float32), -5.0, 5.0)


def draw_point_cells(key, part):
    key = jax.random.fold_in(key, 7)
    key_x, key_y, key_z = jax.random.split(key, 3)
    shape = (N_GX, N_GY, PTS_TILE)
    start_x = jnp.arange(N_GX, dtype=jnp.int32)[:, None, None] * CX
    start_y = jnp.arange(N_GY, dtype=jnp.int32)[None, :, None] * CY
    cell_x = start_x + jax.random.randint(key_x, shape, 0, CX)
    cell_y = start_y + jax.random.randint(key_y, shape, 0, CY)
    cell_z = jax.random.randint(key_z, shape, 0, NZ)
    cell_x = cell_x.at[0, 0, 0].set(0).at[N_GX - 1, N_GY - 1, 0].set(NX - 1)
    cell_y = cell_y.at[0, 0, 0].set(0).at[N_GX - 1, N_GY - 1, 0].set(NY - 1)
    cell_z = cell_z.at[0, 0, 0].set(0).at[N_GX - 1, N_GY - 1, 0].set(NZ - 1)
    return jnp.stack([cell_x, cell_y, cell_z]).astype(jnp.int32)


def draw_point_count(key, part):
    key = jax.random.fold_in(key, 11)
    key_base, key_hot, key_pick = jax.random.split(key, 3)
    base = jax.random.randint(key_base, (N_GX * N_GY,), PTS_TILE // 8, PTS_TILE // 2 + 1)
    hot = jax.random.randint(key_hot, (N_GX * N_GY,), 0, 8) == 0
    counts = jnp.where(hot, PTS_TILE, base)
    chosen = jax.random.randint(key_pick, (), 0, N_GX * N_GY)
    counts = counts.at[chosen].set(PTS_TILE)
    return counts.reshape(N_GX, N_GY).astype(jnp.int32)


def steps_of(rng, shape, cuts, smallest, largest):
    def one(axis_at, parts):
        heights = jax.random.uniform(jax.random.fold_in(jax.random.fold_in(rng, 6), axis_at), (parts,), jnp.float32, smallest / len(cuts), largest / len(cuts))
        return jnp.repeat(jnp.exp(heights), shape[axis_at] // parts).reshape((-1,) + (1,) * (len(shape) - axis_at - 1))

    gain = one(*cuts[0])
    for cut in cuts[1:]:
        gain = gain * one(*cut)
    return gain


def setup_inputs(seed: int = 0) -> dict:
    key_list = jax.random.split(jax.random.key(seed), 7)
    velocity = draw_velocity(jax.random.fold_in(key_list[6], 71), 0)
    point_cells = draw_point_cells(jax.random.fold_in(key_list[6], 71), 0)
    point_offsets = jnp.clip(1.0 * jax.random.uniform(key_list[2], (3, N_GX, N_GY, PTS_TILE), jnp.float32) ** steps_of(key_list[2], (3, N_GX, N_GY, PTS_TILE), ((1, 32), (2, 8)), -0.2, 0.2), 0.0, 1.0)
    point_count = draw_point_count(jax.random.fold_in(key_list[6], 71), 0)
    drag = jnp.clip(jnp.exp(math.log(300.0) - 2.3025851 * jax.random.uniform(key_list[4], (N_GX, N_GY, PTS_TILE), jnp.float32) ** steps_of(key_list[4], (N_GX, N_GY, PTS_TILE), ((0, 32), (1, 8)), -0.2, 0.2)), 30.0, 300.0)
    blade_speed = jnp.clip(0.5 + 1.5 * jax.random.uniform(key_list[5], (N_GX, N_GY, PTS_TILE), jnp.float32) ** steps_of(key_list[5], (N_GX, N_GY, PTS_TILE), ((0, 32), (1, 8)), -0.2, 0.2), 0.5, 2.0)
    return {"velocity": velocity, "point_cells": point_cells, "point_offsets": point_offsets, "point_count": point_count, "drag": drag, "blade_speed": blade_speed}


GAUSS_WIDTH = 1.5
RELAX = 6.0 / 7.0
STEP_DT = 1.0

def line_weights(offset):
    taps = jnp.arange(8, dtype=jnp.float32)
    dist = (taps[None, :] - 3.0 - offset[:, None]) / GAUSS_WIDTH
    bell = jnp.exp(-dist * dist)
    return bell / lax.optimization_barrier(jnp.sum(bell, axis=1, keepdims=True))

def stamp(cells, offsets):
    taps = jnp.arange(8, dtype=jnp.int32)
    weight_x = line_weights(offsets[0])
    weight_y = line_weights(offsets[1])
    weight_z = line_weights(offsets[2])
    weight = weight_x[:, :, None, None] * weight_y[:, None, :, None] * weight_z[:, None, None, :]
    index_x = (cells[0] + 1)[:, None, None, None] + taps[None, :, None, None]
    index_y = (cells[1] + 1)[:, None, None, None] + taps[None, None, :, None]
    index_z = (cells[2] + 1)[:, None, None, None] + taps[None, None, None, :]
    return (weight, index_x, index_y, index_z)

def apply_operator(field, scale):
    padded = jnp.pad(field, 1)
    beside = padded[2:, 1:-1, 1:-1] + padded[:-2, 1:-1, 1:-1]
    beside = beside + padded[1:-1, 2:, 1:-1] + padded[1:-1, :-2, 1:-1]
    beside = beside + padded[1:-1, 1:-1, 2:] + padded[1:-1, 1:-1, :-2]
    return (6.0 * field - beside) * scale

def relax(field, rhs, scale):
    return field + RELAX / (6.0 * scale) * (rhs - apply_operator(field, scale))

def restrict(field):
    sx, sy, sz = field.shape
    return lax.optimization_barrier(jnp.mean(field.reshape(sx // 2, 2, sy // 2, 2, sz // 2, 2), axis=(1, 3, 5)))

def prolong(field):
    return jnp.repeat(jnp.repeat(jnp.repeat(field, 2, axis=0), 2, axis=1), 2, axis=2)

def cycle(field, rhs, level):
    scale = 0.25 ** level
    if level == LEVELS - 1:
        field = relax(jnp.zeros_like(rhs), rhs, scale)
        for sweep in range(COARSE_SWEEPS - 1):
            field = relax(field, rhs, scale)
        return field
    for sweep in range(PRE_SWEEPS):
        field = relax(field, rhs, scale)
    residue = rhs - apply_operator(field, scale)
    coarse = restrict(residue)
    error = cycle(jnp.zeros_like(coarse), coarse, level + 1)
    field = field + prolong(error)
    for sweep in range(POST_SWEEPS):
        field = relax(field, rhs, scale)
    return field

def reference(velocity, point_cells, point_offsets, point_count, drag, blade_speed):
    groups = N_GX * N_GY
    cells = jnp.transpose(point_cells.reshape(3, groups, PTS_TILE), (1, 0, 2))
    offsets = jnp.transpose(point_offsets.reshape(3, groups, PTS_TILE), (1, 0, 2))
    slots = jnp.arange(PTS_TILE, dtype=jnp.int32)
    live = (slots[None, :] < point_count.reshape(groups, 1)).astype(jnp.float32)
    drags = drag.reshape(groups, PTS_TILE)
    blades = blade_speed.reshape(groups, PTS_TILE)
    wide = jnp.pad(velocity, ((0, 0), (4, 4), (4, 4), (4, 4)))

    def sample(item):
        cell, offset, alive, pull, blade = item
        weight, index_x, index_y, index_z = stamp(cell, offset)
        values = wide[:, index_x, index_y, index_z]
        sampled = lax.optimization_barrier(jnp.sum(values * weight[None], axis=(2, 3, 4)))
        speed = jnp.sqrt(lax.optimization_barrier(jnp.sum(sampled * sampled, axis=0)) + blade * blade)
        return -(pull * speed * alive)[None, :] * sampled
    forces = lax.map(sample, (cells, offsets, live, drags, blades))

    def spread(total, item):
        cell, offset, force = item
        weight, index_x, index_y, index_z = stamp(cell, offset)
        total = total.at[:, index_x, index_y, index_z].add(force[:, :, None, None, None] * weight[None])
        return (total, None)
    total, unused = lax.scan(spread, jnp.zeros_like(wide), (cells, offsets, forces))
    pushed = velocity + STEP_DT * total[:, 4:-4, 4:-4, 4:-4]
    flow = jnp.pad(pushed, ((0, 0), (1, 1), (1, 1), (1, 1)))
    rhs = -0.5 * (flow[0, 2:, 1:-1, 1:-1] - flow[0, :-2, 1:-1, 1:-1] + flow[1, 1:-1, 2:, 1:-1] - flow[1, 1:-1, :-2, 1:-1] + flow[2, 1:-1, 1:-1, 2:] - flow[2, 1:-1, 1:-1, :-2])
    pressure = jnp.zeros_like(rhs)
    for turn in range(CYCLES):
        pressure = cycle(pressure, rhs, 0)
    padded = jnp.pad(pressure, 1)
    slope = jnp.stack([padded[2:, 1:-1, 1:-1] - padded[:-2, 1:-1, 1:-1], padded[1:-1, 2:, 1:-1] - padded[1:-1, :-2, 1:-1], padded[1:-1, 1:-1, 2:] - padded[1:-1, 1:-1, :-2]]) * 0.5
    return (pushed - slope, pressure)
```

```python
import functools

import jax
import jax.numpy as jnp
from jax import lax
from jax.experimental import pallas as pl
from jax.experimental.pallas import tpu as pltpu
from jax.sharding import PartitionSpec as P

AXES = ("gx", "gy")
NGX, NGY = 32, 8
W = 32
P_ = 256
F32 = jnp.float32
BF16 = jnp.bfloat16
VMEM = pltpu.VMEM
LIMIT = 40 * 1024 * 1024


def swap(x, fx, fy):
    perm = [(i * NGY + j, fx(i) * NGY + fy(j)) for i in range(NGX) for j in range(NGY)]
    return lax.ppermute(x, AXES, perm)


def same(i):
    return i


def pair(i):
    return i ^ 1


def other(n):
    return lambda i: (i + 1) % n if i % 2 else (i - 1) % n


def swap_gx(a, b):
    return swap(a, pair, same), swap(b, other(NGX), same)


def swap_gy(c, d):
    return swap(c, same, pair), swap(d, same, other(NGY))


def call(kernel, out_shapes, scratch, *args, flops=10_000_000):
    nbytes = sum(a.size * 4 for a in args) + sum(4 * functools.reduce(lambda x, y: x * y, s) for s in out_shapes)
    specs = [pl.BlockSpec(memory_space=pltpu.SMEM)] + [pl.BlockSpec(memory_space=VMEM)] * (len(args) - 1)
    return pl.pallas_call(
        kernel,
        out_shape=[jax.ShapeDtypeStruct(s, F32) for s in out_shapes],
        in_specs=specs,
        out_specs=[pl.BlockSpec(memory_space=VMEM)] * len(out_shapes),
        scratch_shapes=scratch,
        compiler_params=pltpu.CompilerParams(vmem_limit_bytes=LIMIT),
        cost_estimate=pl.CostEstimate(flops=flops, bytes_accessed=nbytes, transcendentals=0),
    )(*args)


def rows(lo, hi, unroll, body):
    n = hi - lo
    main = n // unroll
    if main > 1:

        def step(t, c):
            for u in range(unroll):
                body(lo + t * unroll + u, u)
            return c

        lax.fori_loop(0, main, step, 0)
        lo = lo + main * unroll
    for i in range(lo, hi):
        body(i, (i - lo) % unroll)


def place(info):
    ix, iy = info[0], info[1]
    return ix, iy, ix % 2, iy % 2


def okf(cond):
    return jnp.where(cond, 1.0, 0.0).astype(F32)


def hi_lo(par, a, b):
    return jnp.where(par == 0, a, b), jnp.where(par == 0, b, a)


def lanes(shape=(1, 128)):
    return lax.broadcasted_iota(jnp.int32, shape, len(shape) - 1)


def z_masks(s):
    lane = lanes()
    return okf(lane >= s), okf(lane < 128 - s)


def neighbours(ref, i, v, s, zm, ym=None):
    size = v.shape[0]
    up = pltpu.roll(v, 1, 0)
    down = pltpu.roll(v, size - 1, 0)
    if ym is not None:
        up, down = up * ym[0], down * ym[1]
    low = pltpu.roll(v, s, 1) * zm[0]
    high = pltpu.roll(v, 128 - s, 1) * zm[1]
    return (ref[i - 1] + ref[i + 1]) + (up + down) + (low + high)


def x_in(start, i, size):
    g = start + i
    return okf((g >= 0) & (g < size))


def y_edge(size):
    r = lax.broadcasted_iota(jnp.int32, (size, 1), 0)
    return okf(r > 0), okf(r < size - 1)


def y_domain(size, own, hi, start, total):
    r = lax.broadcasted_iota(jnp.int32, (size, 128), 0)
    g = start + jnp.where(r < own + hi, r, r - size)
    return okf((g >= 0) & (g < total))


def double_sweep(dst, b, lo, hi, s, dom, start, size, ym=None, unroll=2):
    zm = z_masks(s)

    def body(i, u):
        v = b[i]
        c = x_in(start, i, size) * (1.0 / 49.0)
        out = (8.0 * v + neighbours(b, i, v, s, zm, ym)) * c
        if dom is not None:
            out = out * dom[...]
        dst[i] = out

    rows(lo, hi, unroll, body)


def sweep(dst, v_ref, b, lo, hi, s, dom, start, size, ym=None, unroll=2):
    zm = z_masks(s)

    def body(i, u):
        v = v_ref[i]
        c = x_in(start, i, size) * (1.0 / 7.0)
        out = (v + b[i] + neighbours(v_ref, i, v, s, zm, ym)) * c
        if dom is not None:
            out = out * dom[...]
        dst[i] = out

    rows(lo, hi, unroll, body)


def z_pairs(t, s):
    lane = lanes(t.shape)
    return t + jnp.where((lane & s) == 0, pltpu.roll(t, 128 - s, 1), pltpu.roll(t, s, 1))


def restrict_rows(emit, v_ref, b, tmp, klo, khi, base, s, keep, ym=None, unroll=2):
    zm = z_masks(s)

    def body(k, u):
        i = base + 2 * k
        total = None
        for d in range(2):
            v = v_ref[i + d]
            r = b[i + d] - 6.0 * v + neighbours(v_ref, i + d, v, s, zm, ym)
            total = r if total is None else total + r
        tmp[u, 0 : total.shape[0], :] = total
        both = tmp[u, pl.ds(0, keep, stride=2), :] + tmp[u, pl.ds(1, keep, stride=2), :]
        emit(k, u, z_pairs(both, s) * 0.5)

    rows(klo, khi, unroll, body)


def correct(dst, v_ref, e_ref, tmp, klo, khi, base, pieces, size, dom, start, total, get=None, unroll=2):
    def body(k, u):
        e = e_ref[k] if get is None else get(k)
        for at, count, to in pieces:
            part = e[at : at + count]
            tmp[u, pl.ds(to, count, stride=2), :] = part
            tmp[u, pl.ds(to + 1, count, stride=2), :] = part
        wide = tmp[u, 0:size, :]
        for d in range(2):
            i = base + 2 * k + d
            out = v_ref[i] + wide
            if dom is not None:
                out = out * dom[...]
            dst[i] = out * x_in(start, i, total)

    rows(klo, khi, unroll, body)


def split3(x):
    hi = x.astype(BF16)
    lo = (x - hi.astype(F32)).astype(BF16)
    return hi, lo


def dot(a, b):
    return jnp.dot(a, b, preferred_element_type=F32)


def vec(ref, at):
    return jnp.concatenate([ref[at : at + 1, :], ref[at + 1 : at + 2, :]], axis=1)


def tap_norm(off):
    total = jnp.zeros_like(off)
    for k in range(-3, 5):
        u = (k - off) / 1.5
        total = total + jnp.exp(-u * u)
    return 1.0 / total


def taps(coord, cell, off, inv, ok=None):
    d = coord - cell
    u = (d - off) / 1.5
    hit = (d >= -3.0) & (d <= 4.0)
    if ok is not None:
        hit = hit & ok
    return jnp.where(hit, jnp.exp(-u * u) * inv, 0.0)


def row_coord(n, shift):
    return (lax.broadcasted_iota(jnp.int32, (n, 1), 0) + shift).astype(F32)


def cyc_coord(n, split):
    r = lax.broadcasted_iota(jnp.int32, (n, 1), 0)
    return jnp.where(r < split, r, r - n).astype(F32)


def pack_gy(info, vel, pts, c_out, d_out):
    ix, iy, px, py = place(info)

    def body(t, u):
        c = t // W
        x = t - c * W
        top = vel[c, x, W - 4 : W, :]
        bottom = vel[c, x, 0:4, :]
        to_hi, to_lo = top, bottom
        c_out[t] = jnp.where(py == 0, to_hi, to_lo)
        d_out[t] = jnp.where(py == 0, to_lo, to_hi)

    rows(0, 3 * W, 4, body)
    for k in range(3):
        c_out[3 * W + k] = pts[4 * k : 4 * k + 4, :]
        d_out[3 * W + k] = pts[4 * k : 4 * k + 4, :]


def pack_gx(info, vel, pts, c_in, d_in, a_out, b_out):
    ix, iy, px, py = place(info)
    ok_hi, ok_lo = okf(iy < NGY - 1), okf(iy > 0)
    off_a = jnp.where(px == 0, W - 4, 0)
    off_b = W - 4 - off_a
    for out, off in ((a_out, off_a), (b_out, off_b)):
        for c in range(3):
            for k in range(4):
                x = off + k
                e = c * 4 + k
                hi, lo = hi_lo(py, c_in[c * W + x], d_in[c * W + x])
                out[e, 0:W, :] = vel[c, x]
                out[e, W : W + 4, :] = hi * ok_hi
                out[e, W + 4 : W + 8, :] = lo * ok_lo
        out[12, 0:12, :] = pts[...]
        for k in range(3):
            hi, lo = hi_lo(py, c_in[3 * W + k], d_in[3 * W + k])
            out[12, 12 + 4 * k : 16 + 4 * k, :] = hi
            out[12, 24 + 4 * k : 28 + 4 * k, :] = lo
        out[12, 36:40, :] = jnp.zeros((4, 128), F32)


def force_kernel(info, vel, pts, sect, c_in, d_in, a_in, b_in, g_out, f_out, c_out, d_out, wide, wxs, dxs, acc):
    ix, iy, px, py = place(info)
    ok_hi, ok_lo = okf(iy < NGY - 1), okf(iy > 0)
    okx_hi, okx_lo = okf(ix < NGX - 1), okf(ix > 0)

    def fill(t, u):
        c = t // W
        x = t - c * W
        hi, lo = hi_lo(py, c_in[t], d_in[t])
        wide[c, x + 4, 0:W, :] = vel[c, x]
        wide[c, x + 4, W : W + 4, :] = hi * ok_hi
        wide[c, x + 4, W + 4 : W + 8, :] = lo * ok_lo

    rows(0, 3 * W, 2, fill)
    for c in range(3):
        for k in range(4):
            e = c * 4 + k
            hi, lo = hi_lo(px, a_in[e], b_in[e])
            wide[c, W + 4 + k] = hi * okx_hi
            wide[c, k] = lo * okx_lo

    start_x = (ix * W).astype(F32)
    start_y = (iy * W).astype(F32)
    cx = vec(pts, 0) - start_x
    cy = vec(pts, 2) - start_y
    cz = vec(pts, 4)
    ox, oy, oz = vec(pts, 6), vec(pts, 8), vec(pts, 10)
    nx, ny, nz = tap_norm(ox), tap_norm(oy), tap_norm(oz)
    z = row_coord(128, 0)

    wz = taps(z, cz, oz, nz)
    wz_hi, wz_lo = split3(wz)
    wz3 = jnp.concatenate([wz_hi, wz_lo, wz_hi], axis=0)
    wxs[0:40, :] = taps(row_coord(40, -4), cx, ox, nx)
    wy40 = taps(cyc_coord(40, 36), cy, oy, ny)
    for c in range(3):
        acc[c] = jnp.zeros((40, P_), F32)

    def sample(t, carry):
        for c in range(3):
            part = wide[c, pl.ds(t * 8, 8)].reshape(320, 128)
            hi, lo = split3(part)
            r = dot(jnp.concatenate([hi, hi, lo], axis=1), wz3).reshape(8, 40, P_)
            s = acc[c]
            for k in range(8):
                s = s + r[k] * wxs[pl.ds(t * 8 + k, 1), :]
            acc[c] = s
        return carry

    lax.fori_loop(0, 5, sample, 0)
    sampled = [jnp.sum(acc[c] * wy40, axis=0, keepdims=True) for c in range(3)]
    drag, blade = vec(sect, 0), vec(sect, 2)
    slot = lax.broadcasted_iota(jnp.int32, (1, P_), 1)
    live = okf(slot < info[2])
    speed = jnp.sqrt(sampled[0] * sampled[0] + sampled[1] * sampled[1] + sampled[2] * sampled[2] + blade * blade)
    pull = -(drag * speed * live)
    force = [pull * s for s in sampled]
    for c in range(3):
        f_out[2 * c : 2 * c + 1, :] = force[c][:, 0:128]
        f_out[2 * c + 1 : 2 * c + 2, :] = force[c][:, 128:256]
    f_out[6:8, :] = jnp.zeros((2, 128), F32)

    def axis_taps(coord, cell, off, inv, start, size):
        def at(shift):
            q = coord + shift
            ok = (q + start >= 0.0) & (q + start < size)
            return taps(q, cell, off, inv, ok)

        return at(0.0), at(1.0) - at(-1.0)

    wx, dx = axis_taps(row_coord(48, -5), cx, ox, nx, start_x, float(W * NGX))
    wy, dy = axis_taps(cyc_coord(48, 40), cy, oy, ny, start_y, float(W * NGY))
    wzz, dz = axis_taps(z, cz, oz, nz, 0.0, 128.0)
    wxs[...] = wx
    dxs[...] = dx
    r1_hi, r1_lo = split3(-0.5 * wzz.T)
    r2_hi, r2_lo = split3(-0.5 * dz.T)
    right = jnp.concatenate([r1_hi, r2_hi, r1_lo, r2_lo, r1_hi, r2_hi], axis=0)
    fy_dy = force[1] * dy
    fx_wy = force[0] * wy
    fz_wy = force[2] * wy

    def spread(t, carry):
        l1, l2 = [], []
        for k in range(7):
            i = t * 7 + k
            row_w = wxs[pl.ds(i, 1), :]
            row_d = dxs[pl.ds(i, 1), :]
            l1.append(row_d * fx_wy + row_w * fy_dy)
            l2.append(row_w * fz_wy)
        l1_hi, l1_lo = split3(jnp.concatenate(l1, axis=0))
        l2_hi, l2_lo = split3(jnp.concatenate(l2, axis=0))
        left = jnp.concatenate([l1_hi, l2_hi, l1_hi, l2_hi, l1_lo, l2_lo], axis=1)
        g_out[pl.ds(t * 7, 7)] = dot(left, right).reshape(7, 48, 128)
        return carry

    lax.fori_loop(0, 6, spread, 0)

    zm = z_masks(1)

    def rhs(x, u):
        vx = wide[0, x + 5, 0:W, :] - wide[0, x + 3, 0:W, :]
        vy = wide[1, x + 4]
        vy = pltpu.roll(vy, 39, 0)[0:W] - pltpu.roll(vy, 1, 0)[0:W]
        vz = wide[2, x + 4, 0:W, :]
        vz = pltpu.roll(vz, 127, 1) * zm[1] - pltpu.roll(vz, 1, 1) * zm[0]
        g_out[x + 5, 0:W, :] = g_out[x + 5, 0:W, :] - 0.5 * (vx + vy + vz)

    rows(0, W, 2, rhs)

    def pack(i, u):
        g = g_out[i]
        to_hi = g[24:40]
        to_lo = jnp.concatenate([g[40:48], g[0:8]], axis=0)
        c_out[i] = jnp.where(py == 0, to_hi, to_lo)
        d_out[i] = jnp.where(py == 0, to_lo, to_hi)

    rows(0, 42, 2, pack)


def merge_g(info, g, c_in, d_in, h_out, a_out, b_out):
    ix, iy, px, py = place(info)
    ok_hi, ok_lo = okf(iy < NGY - 1), okf(iy > 0)

    def body(i, u):
        hi, lo = hi_lo(py, c_in[i], d_in[i])
        hi, lo = hi * ok_hi, lo * ok_lo
        v = g[i]
        h_out[i, 0:8, :] = v[0:8] + lo[8:16]
        h_out[i, 8:24, :] = v[8:24]
        h_out[i, 24:40, :] = v[24:40] + hi
        h_out[i, 40:48, :] = v[40:48] + lo[0:8]

    rows(0, 42, 2, body)
    off_a = jnp.where(px == 0, 31, 0)
    off_b = 31 - off_a

    def pack(k, u):
        a_out[k] = h_out[off_a + k]
        b_out[k] = h_out[off_b + k]

    rows(0, 11, 2, pack)


def emit_level1(c_out, tmp1, v2, b, tmp):
    lane = lanes((16, 128))

    def emit(k, u, r):
        tmp1[k] = r

    restrict_rows(emit, v2, b, tmp, 0, 16, 6, 1, 16)
    for k in range(8):
        c_out[k] = jnp.where((lane & 1) == 0, tmp1[2 * k], tmp1[2 * k + 1])


def down0(info, h, a_in, b_in, f, b_out, v_out, c_out, dom, tmp, tmp1):
    ix, iy, px, py = place(info)
    okx_hi, okx_lo = okf(ix < NGX - 1), okf(ix > 0)
    dom[...] = y_domain(48, W, 8, iy * W, W * NGY)
    start = ix * W - 6

    def inner(i, u):
        b_out[i] = h[i - 1] * dom[...] * x_in(start, i, W * NGX)

    rows(1, 43, 2, inner)
    zero = jnp.zeros((48, 128), F32)
    b_out[0] = zero
    b_out[43] = zero

    def rim(k, u):
        hi, lo = hi_lo(px, a_in[k], b_in[k])
        b_out[k] = b_out[k] + lo * dom[...] * (okx_lo * x_in(start, k, W * NGX))
        j = k + 33
        b_out[j] = b_out[j] + hi * dom[...] * (okx_hi * x_in(start, j, W * NGX))

    rows(0, 11, 1, rim)
    v_out[0] = zero
    v_out[43] = zero
    double_sweep(v_out, b_out, 1, 43, 1, dom, start, W * NGX)
    emit_level1(c_out, tmp1, v_out, b_out, tmp)
    c_out[8, 0:8, :] = f[...]
    c_out[8, 8:16, :] = jnp.zeros((8, 128), F32)


def pack1_gx(info, own, c_in, d_in, a_out, b_out):
    ix, iy, px, py = place(info)
    ok_hi, ok_lo = okf(iy < NGY - 1), okf(iy > 0)
    off_a = jnp.where(px == 0, 3, 0)
    off_b = 3 - off_a
    for out, off in ((a_out, off_a), (b_out, off_b)):
        for k in range(6):
            e = off + k if k < 5 else 8
            hi, lo = hi_lo(py, c_in[e], d_in[e])
            out[k, 0:16, :] = own[e]
            out[k, 16:32, :] = hi * ok_hi
            out[k, 32:48, :] = lo * ok_lo


def down1(info, own, c_in, d_in, a_in, b_in, b1, v1, b2, v2, packed, dom1, dom2, tmp, tmp3):
    ix, iy, px, py = place(info)
    ok_hi, ok_lo = okf(iy < NGY - 1), okf(iy > 0)
    okx_hi, okx_lo = okf(ix < NGX - 1), okf(ix > 0)
    n1x, n1y = W * NGX // 2, W * NGY // 2
    dom1[...] = y_domain(48, 16, 16, iy * 16, n1y)
    dom2[...] = y_domain(24, 8, 8, iy * 8, n1y // 2)
    even = (lanes((48, 128)) & 1) == 0

    def unpack(at, p):
        b1[at] = jnp.where(even, p, pltpu.roll(p, 1, 1))
        b1[at + 1] = jnp.where(even, pltpu.roll(p, 127, 1), p)

    for k in range(8):
        hi, lo = hi_lo(py, c_in[k], d_in[k])
        unpack(10 + 2 * k, jnp.concatenate([own[k], hi * ok_hi, lo * ok_lo], axis=0))
    for k in range(5):
        hi, lo = hi_lo(px, a_in[k], b_in[k])
        unpack(2 * k, lo * okx_lo)
        unpack(26 + 2 * k, hi * okx_hi)
    zero1 = jnp.zeros((48, 128), F32)
    v1[0] = zero1
    v1[35] = zero1
    start1 = ix * 16 - 10
    double_sweep(v1, b1, 1, 35, 2, dom1, start1, n1x)
    start2 = ix * 8 - 4

    def emit2(k, u, r):
        b2[k] = r * dom2[...] * x_in(start2, k, n1x // 2)

    restrict_rows(emit2, v1, b1, tmp, 0, 16, 2, 2, 24)
    zero2 = jnp.zeros((24, 128), F32)
    v2[0] = zero2
    v2[15] = zero2
    double_sweep(v2, b2, 1, 15, 4, dom2, start2, n1x // 2)

    def emit3(k, u, r):
        tmp3[k] = r

    restrict_rows(emit3, v2, b2, tmp, 0, 4, 4, 4, 8)
    row = lax.broadcasted_iota(jnp.int32, (8, 128), 0)
    lane = lanes((8, 128)) & 7
    first = okf((lane == row) & (row < 4))
    second = okf((lane == row + 4) & (row < 4))
    for q in range(2):
        s = tmp3[2 * q] * first + tmp3[2 * q + 1] * second
        packed[q : q + 1, :] = jnp.sum(s, axis=0, keepdims=True)


def coarse_up(info, g, b1, v1, b2, v2, s):
    ix, iy, px, py = place(info)
    n3x = NGX * 4

    def load(d, u):
        at = ix - 7 + d
        ok = okf((at >= 0) & (at < NGX))
        at = jnp.clip(at, 0, NGX - 1)
        base = d * 16
        s.px[pl.ds(pl.multiple_of(base, 8), 8), :] = g[at, pl.ds(0, 8, stride=2), :] * ok
        s.px[pl.ds(pl.multiple_of(base + 8, 8), 8), :] = g[at, pl.ds(1, 8, stride=2), :] * ok

    rows(0, 15, 1, load)
    src = lax.broadcasted_iota(jnp.int32, (128, 1024), 0)
    dst = lax.broadcasted_iota(jnp.int32, (128, 1024), 1)
    pick = okf(src == ((dst & 127) >> 3) * 8 + (dst >> 7)).astype(BF16)
    x = s.px[...]
    x_hi, x_lo = split3(x)
    x_lo2 = (x - x_hi.astype(F32) - x_lo.astype(F32)).astype(BF16)
    s.pu[...] = dot(x_hi, pick) + dot(x_lo, pick) + dot(x_lo2, pick)

    def place3(d, u):
        for q in range(2):
            for j in range(8):
                part = s.pu[pl.ds(pl.multiple_of(d * 16 + q * 8, 8), 8), j * 128 : (j + 1) * 128]
                s.b3[d * 4 + 2 * q + (j >> 2), pl.ds(j & 3, 8, stride=4), :] = part

    rows(0, 15, 1, place3)
    e3, e4, e5 = y_edge(32), y_edge(16), y_edge(8)
    start3, start4, start5 = (ix - 7) * 4, (ix - 7) * 2, ix - 7
    z3, z4, z5 = jnp.zeros((32, 128), F32), jnp.zeros((16, 128), F32), jnp.zeros((8, 128), F32)
    for r, z, n in ((s.v3, z3, 60), (s.b4, z4, 30), (s.v4, z4, 30), (s.b5, z5, 15), (s.v5, z5, 15), (s.w5, z5, 15)):
        r[0] = z
        r[n - 1] = z
    double_sweep(s.v3, s.b3, 1, 59, 8, None, start3, n3x, e3)

    def emit4(k, u, r):
        s.b4[k] = r * x_in(start4, k, n3x // 2)

    restrict_rows(emit4, s.v3, s.b3, s.tmp, 1, 29, 0, 8, 16, e3)
    double_sweep(s.v4, s.b4, 1, 29, 16, None, start4, n3x // 2, e4)

    def emit5(k, u, r):
        s.b5[k] = r * x_in(start5, k, NGX)

    restrict_rows(emit5, s.v4, s.b4, s.tmp, 1, 14, 0, 16, 8, e4)
    double_sweep(s.v5, s.b5, 1, 14, 32, None, start5, NGX, e5)
    sweep(s.w5, s.v5, s.b5, 1, 14, 32, None, start5, NGX, e5)
    sweep(s.v5, s.w5, s.b5, 1, 14, 32, None, start5, NGX, e5)

    correct(s.w4, s.v4, s.v5, s.tmp, 5, 10, 0, ((0, 8, 0),), 16, None, start4, n3x // 2)
    sweep(s.v4, s.w4, s.b4, 11, 19, 16, None, start4, n3x // 2, e4)
    correct(s.w3, s.v3, s.v4, s.tmp, 12, 18, 0, ((0, 16, 0),), 32, None, start3, n3x)
    sweep(s.v3, s.w3, s.b3, 26, 34, 8, None, start3, n3x, e3)

    s.dom2[...] = y_domain(24, 8, 8, iy * 8, NGY * 8)
    s.dom1[...] = y_domain(48, 16, 16, iy * 16, NGY * 16)
    turn = lax.rem(32 - 4 * iy, 32)

    def shifted(k):
        return pltpu.roll(s.v3[k + 26], turn, 0)

    start2, start1 = ix * 8 - 4, ix * 16 - 10
    n2x, n1x = n3x * 2, n3x * 4
    correct(s.w2, v2, None, s.tmp, 0, 8, 0, ((0, 8, 0), (28, 4, 16)), 24, s.dom2, start2, n2x, shifted)
    sweep(s.e2, s.w2, b2, 2, 14, 4, s.dom2, start2, n2x)
    correct(s.w1, v1, s.e2, s.tmp, 2, 14, 2, ((0, 24, 0),), 48, s.dom1, start1, n1x)
    sweep(s.e1, s.w1, b1, 7, 29, 2, s.dom1, start1, n1x)


class Bag:
    pass


COARSE = (
    ("px", (240, 128)),
    ("pu", (240, 1024)),
    ("b3", (60, 32, 128)),
    ("v3", (60, 32, 128)),
    ("w3", (60, 32, 128)),
    ("b4", (30, 16, 128)),
    ("v4", (30, 16, 128)),
    ("w4", (30, 16, 128)),
    ("b5", (15, 8, 128)),
    ("v5", (15, 8, 128)),
    ("w5", (15, 8, 128)),
    ("w2", (16, 24, 128)),
    ("e2", (16, 24, 128)),
    ("w1", (36, 48, 128)),
    ("e1", (36, 48, 128)),
    ("w0", (44, 48, 128)),
    ("x0", (44, 48, 128)),
    ("dom0", (48, 128)),
    ("dom1", (48, 128)),
    ("dom2", (24, 128)),
    ("tmp", (4, 48, 128)),
    ("tmp1", (16, 16, 128)),
)
COARSE_SCRATCH = [pltpu.VMEM(shape, F32) for name, shape in COARSE]


def bag(refs):
    s = Bag()
    for (name, shape), ref in zip(COARSE, refs):
        setattr(s, name, ref)
    return s


PIECES0 = ((0, 20, 0), (44, 4, 40))


def middle(info, g, b0, v0, b1, v1, b2, v2, v_out, c_out, *scratch):
    s = bag(scratch)
    ix, iy, px, py = place(info)
    coarse_up(info, g, b1, v1, b2, v2, s)
    s.dom0[...] = y_domain(48, W, 8, iy * W, W * NGY)
    start, size = ix * W - 6, W * NGX
    correct(s.w0, v0, s.e1, s.tmp, 7, 29, -14, PIECES0, 48, s.dom0, start, size)
    sweep(s.x0, s.w0, b0, 2, 42, 1, s.dom0, start, size)
    sweep(s.w0, s.x0, b0, 3, 41, 1, s.dom0, start, size)
    sweep(v_out, s.w0, b0, 4, 40, 1, s.dom0, start, size)
    zero = jnp.zeros((48, 128), F32)
    for i in (0, 1, 2, 3, 40, 41, 42, 43):
        v_out[i] = zero
    emit_level1(c_out, s.tmp1, v_out, b0, s.tmp)


def final(info, g, b0, v0, b1, v1, b2, v2, pushed, vel_out, p_out, *scratch):
    s = bag(scratch)
    ix, iy, px, py = place(info)
    coarse_up(info, g, b1, v1, b2, v2, s)
    s.dom0[...] = y_domain(48, W, 8, iy * W, W * NGY)
    start, size = ix * W - 6, W * NGX
    correct(s.w0, v0, s.e1, s.tmp, 9, 27, -14, PIECES0, 48, s.dom0, start, size)
    sweep(s.x0, s.w0, b0, 5, 39, 1, s.dom0, start, size)
    zm = z_masks(1)

    def body(x, u):
        p = s.x0[x + 6]
        own = p[0:W]
        p_out[x] = own
        gx = s.x0[x + 7, 0:W, :] - s.x0[x + 5, 0:W, :]
        gy = pltpu.roll(p, 47, 0)[0:W] - pltpu.roll(p, 1, 0)[0:W]
        gz = pltpu.roll(own, 127, 1) * zm[1] - pltpu.roll(own, 1, 1) * zm[0]
        vel_out[0, x] = pushed[0, x] - 0.5 * gx
        vel_out[1, x] = pushed[1, x] - 0.5 * gy
        vel_out[2, x] = pushed[2, x] - 0.5 * gz

    rows(0, W, 2, body)


def push_kernel(info, vel, pts, f, c_in, d_in, a_in, b_in, c1, d1, a1, b1, out, wxs, pbuf):
    ix, iy, px, py = place(info)
    ok = {-1: (okf(ix > 0), okf(iy > 0)), 0: (1.0, 1.0), 1: (okf(ix < NGX - 1), okf(iy < NGY - 1))}
    start_x = (ix * W).astype(F32)
    start_y = (iy * W).astype(F32)

    def store(slot, points, forces):
        pbuf[slot, 0:12, :] = points
        pbuf[slot, 12:18, :] = forces

    def cat3(ref):
        return jnp.concatenate([ref[3 * W], ref[3 * W + 1], ref[3 * W + 2]], axis=0)

    hi, lo = hi_lo(py, cat3(c_in), cat3(d_in))
    fhi, flo = hi_lo(py, c1[8, 0:6, :], d1[8, 0:6, :])
    store(0, pts[...], f[0:6, :])
    store(1, hi, fhi)
    store(2, lo, flo)
    xhi, xlo = hi_lo(px, a_in[12], b_in[12])
    ghi, glo = hi_lo(px, a1[5], b1[5])
    for n, (q, fq) in enumerate(((xhi, ghi), (xlo, glo))):
        for m in range(3):
            store(3 + 3 * n + m, q[12 * m : 12 * m + 12], fq[16 * m : 16 * m + 6])

    order = ((0, 0), (0, 1), (0, -1), (1, 0), (1, 1), (1, -1), (-1, 0), (-1, 1), (-1, -1))
    for slot, (ox_, oy_) in enumerate(order):
        q = pbuf.at[slot]
        cx, cy, cz = vec(q, 0) - start_x, vec(q, 2) - start_y, vec(q, 4)
        ox, oy, oz = vec(q, 6), vec(q, 8), vec(q, 10)
        keep = ok[ox_][0] * ok[oy_][1]
        force = [vec(q, 12 + 2 * c) * keep for c in range(3)]
        wxs[...] = taps(row_coord(32, 0), cx, ox, tap_norm(ox))
        y0, yn = {0: (0, 32), 1: (24, 8), -1: (0, 8)}[oy_]
        wy = taps(row_coord(yn, y0), cy, oy, tap_norm(oy))
        wz = taps(row_coord(128, 0), cz, oz, tap_norm(oz)).T
        r_hi, r_lo = split3(wz)
        right = jnp.concatenate([r_hi, r_lo, r_hi], axis=0)
        fy = [force[c] * wy for c in range(3)]
        x0, xn = {0: (0, 32), 1: (28, 4), -1: (0, 4)}[ox_]
        step = min(xn, 4 if oy_ == 0 else 16)

        def spread(t, carry, x0=x0, step=step, fy=fy, right=right, y0=y0, yn=yn, slot=slot):
            at = x0 + t * step
            left = []
            for k in range(step):
                row = wxs[pl.ds(at + k, 1), :]
                left += [row * fy[c] for c in range(3)]
            hi, lo = split3(jnp.concatenate(left, axis=0))
            r = dot(jnp.concatenate([hi, hi, lo], axis=1), right).reshape(step, 3, yn, 128)
            for k in range(step):
                for c in range(3):
                    base = vel if slot == 0 else out
                    out[c, at + k, y0 : y0 + yn, :] = base[c, at + k, y0 : y0 + yn, :] + r[k, c]
            return carry

        lax.fori_loop(0, xn // step, spread, 0)


def gather3(packed):
    everyone = jnp.broadcast_to(packed[None], (NGX * NGY, 2, 128))
    return lax.all_to_all(everyone, AXES, 0, 0, tiled=True).reshape(NGX, 16, 128)


def level_one(info, own):
    c1, d1 = swap_gy(own, own)
    a1, b1 = call(pack1_gx, [(6, 48, 128)] * 2, [], info, own, c1, d1)
    a1, b1 = swap_gx(a1, b1)
    outs = call(
        down1,
        [(36, 48, 128), (36, 48, 128), (16, 24, 128), (16, 24, 128), (2, 128)],
        [VMEM((48, 128), F32), VMEM((24, 128), F32), VMEM((4, 48, 128), F32), VMEM((4, 8, 128), F32)],
        info, own, c1, d1, a1, b1,
    )
    return (c1, d1, a1, b1), outs[:4], gather3(outs[4])


def per_device(velocity, point_cells, point_offsets, point_count, drag, blade_speed):
    info = jnp.stack([lax.axis_index("gx"), lax.axis_index("gy"), point_count.reshape(())]).astype(jnp.int32)
    pts = jnp.concatenate([point_cells.astype(F32).reshape(6, 128), point_offsets.reshape(6, 128)], axis=0)
    sect = jnp.concatenate([drag.reshape(2, 128), blade_speed.reshape(2, 128)], axis=0)

    c0, d0 = call(pack_gy, [(99, 4, 128)] * 2, [], info, velocity, pts)
    c0, d0 = swap_gy(c0, d0)
    a0, b0 = call(pack_gx, [(13, 40, 128)] * 2, [], info, velocity, pts, c0, d0)
    a0, b0 = swap_gx(a0, b0)
    g, f, cg, dg = call(
        force_kernel,
        [(42, 48, 128), (8, 128), (42, 16, 128), (42, 16, 128)],
        [VMEM((3, 40, 40, 128), F32), VMEM((48, P_), F32), VMEM((48, P_), F32), VMEM((3, 40, P_), F32)],
        info, velocity, pts, sect, c0, d0, a0, b0,
    )
    cg, dg = swap_gy(cg, dg)
    h, ag, bg = call(merge_g, [(42, 48, 128), (11, 48, 128), (11, 48, 128)], [], info, g, cg, dg)
    ag, bg = swap_gx(ag, bg)
    rhs, v0, own1 = call(
        down0,
        [(44, 48, 128), (44, 48, 128), (9, 16, 128)],
        [VMEM((48, 128), F32), VMEM((4, 48, 128), F32), VMEM((16, 16, 128), F32)],
        info, h, ag, bg, f,
    )
    (c1, d1, a1, b1), levels, gathered = level_one(info, own1)
    (pushed,) = call(
        push_kernel,
        [(3, W, W, 128)],
        [VMEM((32, P_), F32), VMEM((9, 24, 128), F32)],
        info, velocity, pts, f, c0, d0, a0, b0, c1, d1, a1, b1,
    )
    v0, own1 = call(middle, [(44, 48, 128), (8, 16, 128)], COARSE_SCRATCH, info, gathered, rhs, v0, *levels)
    own1 = jnp.concatenate([own1, jnp.zeros((1, 16, 128), F32)], axis=0)
    unused, levels, gathered = level_one(info, own1)
    vel_out, p_out = call(
        final, [(3, W, W, 128), (W, W, 128)], COARSE_SCRATCH, info, gathered, rhs, v0, *levels, pushed
    )
    return vel_out, p_out


def solution(mesh):
    placed = (
        P(None, "gx", "gy", None),
        P(None, "gx", "gy", None),
        P(None, "gx", "gy", None),
        P("gx", "gy"),
        P("gx", "gy", None),
        P("gx", "gy", None),
    )
    return jax.shard_map(
        per_device,
        mesh=mesh,
        in_specs=placed,
        out_specs=(P(None, "gx", "gy", None), P("gx", "gy", None)),
        check_vma=False,
    )
```

```python
import functools

import jax
import jax.numpy as jnp
from jax import lax
from jax.experimental import pallas as pl
from jax.experimental.pallas import tpu as pltpu
from jax.sharding import PartitionSpec as P

AXES = ("gx", "gy")
NGX, NGY = 32, 8
W = 32
P_ = 256
F32 = jnp.float32
BF16 = jnp.bfloat16
VMEM = pltpu.VMEM
LIMIT = 24 * 1024 * 1024
WHOLE = 63 * 1024 * 1024


def swap(x, fx, fy):
    perm = [(i * NGY + j, fx(i) * NGY + fy(j)) for i in range(NGX) for j in range(NGY)]
    return lax.ppermute(x, AXES, perm)


def same(i):
    return i


def pair(i):
    return i ^ 1


def other(n):
    return lambda i: (i + 1) % n if i % 2 else (i - 1) % n


def swap_gx(a, b):
    return swap(a, pair, same), swap(b, other(NGX), same)


def swap_gy(c, d):
    return swap(c, same, pair), swap(d, same, other(NGY))


class Late:
    def __init__(self, copy, ref):
        self.copy, self.ref, self.done = copy, ref, False

    def get(self):
        if not self.done:
            self.copy.wait()
            self.done = True
        return self.ref


def use(x):
    return x.get() if isinstance(x, Late) else x


class Early:
    def __init__(self, copy, ref):
        self.copy, self.ref, self.sent = copy, ref, False

    def flush(self):
        if not self.sent:
            self.copy.start()
            self.sent = True


def call(kernel, out_shapes, scratch, *args, late=(), early=()):
    nbytes = sum(a.size * 4 for a in args) + sum(4 * functools.reduce(lambda x, y: x * y, s) for s in out_shapes)
    n_in, n_out = len(args), len(out_shapes)

    def body(*refs):
        ins, outs = list(refs[:n_in]), list(refs[n_in : n_in + n_out])
        rest = refs[n_in + n_out :]
        own, rest = rest[: len(scratch)], rest[len(scratch) :]
        if late or early:
            bufs, sems = rest[:-1], rest[-1]
        for n, at in enumerate(late):
            copy = pltpu.make_async_copy(ins[at], bufs[n], sems.at[n])
            copy.start()
            ins[at] = Late(copy, bufs[n])
        for n, at in enumerate(early):
            k = len(late) + n
            outs[at] = Early(pltpu.make_async_copy(bufs[k], outs[at], sems.at[k]), bufs[k])
        kernel(*ins, *outs, *own)
        for at in late:
            use(ins[at])
        for at in early:
            outs[at].flush()
        for at in early:
            outs[at].copy.wait()

    specs = [pl.BlockSpec(memory_space=pltpu.SMEM)] + [
        pl.BlockSpec(memory_space=pltpu.HBM if n in late else VMEM) for n in range(1, n_in)
    ]
    extra = [VMEM(args[n].shape, args[n].dtype) for n in late] + [VMEM(out_shapes[n], F32) for n in early]
    if extra:
        extra.append(pltpu.SemaphoreType.DMA((len(extra),)))
    return pl.pallas_call(
        body,
        out_shape=[jax.ShapeDtypeStruct(s, F32) for s in out_shapes],
        in_specs=specs,
        out_specs=[pl.BlockSpec(memory_space=pltpu.HBM if n in early else VMEM) for n in range(n_out)],
        scratch_shapes=list(scratch) + extra,
        compiler_params=pltpu.CompilerParams(vmem_limit_bytes=WHOLE if late else LIMIT),
        cost_estimate=pl.CostEstimate(flops=10_000_000, bytes_accessed=nbytes, transcendentals=0),
    )(*args)


def rows(lo, hi, unroll, body):
    n = hi - lo
    main = n // unroll if unroll < n else 0
    if main > 1:

        def step(t, c):
            for u in range(unroll):
                body(lo + t * unroll + u, u)
            return c

        lax.fori_loop(0, main, step, 0)
        lo = lo + main * unroll
    for i in range(lo, hi):
        body(i, i - lo)


def place(info):
    ix, iy = info[0], info[1]
    return ix, iy, ix % 2, iy % 2


def okf(cond):
    return jnp.where(cond, 1.0, 0.0).astype(F32)


def hi_lo(par, a, b):
    return jnp.where(par == 0, a, b), jnp.where(par == 0, b, a)


def lanes(shape=(1, 128)):
    return lax.broadcasted_iota(jnp.int32, shape, len(shape) - 1)


def z_masks(s):
    lane = lanes()
    return okf(lane >= s), okf(lane < 128 - s)


def neighbours(ref, i, v, s, zm, ym=None):
    size = v.shape[0]
    up = pltpu.roll(v, 1, 0)
    down = pltpu.roll(v, size - 1, 0)
    if ym is not None:
        up, down = up * ym[0], down * ym[1]
    low = pltpu.roll(v, s, 1) * zm[0]
    high = pltpu.roll(v, 128 - s, 1) * zm[1]
    return (ref[i - 1] + ref[i + 1]) + (up + down) + (low + high)


def x_in(start, i, size):
    g = start + i
    return okf((g >= 0) & (g < size))


def y_edge(size):
    r = lax.broadcasted_iota(jnp.int32, (size, 1), 0)
    return okf(r > 0), okf(r < size - 1)


def y_domain(size, own, hi, start, total):
    r = lax.broadcasted_iota(jnp.int32, (size, 128), 0)
    g = start + jnp.where(r < own + hi, r, r - size)
    return okf((g >= 0) & (g < total))


def double_sweep(dst, b, lo, hi, s, dom, start, size, ym=None, unroll=64):
    zm = z_masks(s)

    def body(i, u):
        v = b[i]
        c = x_in(start, i, size) * (1.0 / 49.0)
        out = (8.0 * v + neighbours(b, i, v, s, zm, ym)) * c
        if dom is not None:
            out = out * dom[...]
        dst[i] = out

    rows(lo, hi, unroll, body)


def sweep(dst, v_ref, b, lo, hi, s, dom, start, size, ym=None, unroll=64):
    zm = z_masks(s)

    def body(i, u):
        v = v_ref[i]
        c = x_in(start, i, size) * (1.0 / 7.0)
        out = (v + b[i] + neighbours(v_ref, i, v, s, zm, ym)) * c
        if dom is not None:
            out = out * dom[...]
        dst[i] = out

    rows(lo, hi, unroll, body)


def z_pairs(t, s):
    lane = lanes(t.shape)
    return t + jnp.where((lane & s) == 0, pltpu.roll(t, 128 - s, 1), pltpu.roll(t, s, 1))


def restrict_rows(emit, v_ref, b, tmp, klo, khi, base, s, keep, ym=None, unroll=64):
    zm = z_masks(s)

    def first(k, u):
        i = base + 2 * k
        total = None
        for d in range(2):
            v = v_ref[i + d]
            r = b[i + d] - 6.0 * v + neighbours(v_ref, i + d, v, s, zm, ym)
            total = r if total is None else total + r
        tmp[u, 0 : total.shape[0], :] = total

    def second(k, u):
        both = tmp[u, pl.ds(0, keep, stride=2), :] + tmp[u, pl.ds(1, keep, stride=2), :]
        emit(k, u, z_pairs(both, s) * 0.5)

    rows(klo, khi, unroll, first)
    rows(klo, khi, unroll, second)


def correct(dst, v_ref, e_ref, tmp, klo, khi, base, pieces, size, dom, start, total, get=None, unroll=64):
    def first(k, u):
        e = e_ref[k] if get is None else get(k)
        for at, count, to in pieces:
            part = e[at : at + count]
            tmp[u, pl.ds(to, count, stride=2), :] = part
            tmp[u, pl.ds(to + 1, count, stride=2), :] = part

    def second(k, u):
        wide = tmp[u, 0:size, :]
        for d in range(2):
            i = base + 2 * k + d
            out = v_ref[i] + wide
            if dom is not None:
                out = out * dom[...]
            dst[i] = out * x_in(start, i, total)

    rows(klo, khi, unroll, first)
    rows(klo, khi, unroll, second)


def split3(x):
    hi = x.astype(BF16)
    lo = (x - hi.astype(F32)).astype(BF16)
    return hi, lo


def dot(a, b):
    return jnp.dot(a, b, preferred_element_type=F32)


def vec(ref, at):
    return jnp.concatenate([ref[at : at + 1, :], ref[at + 1 : at + 2, :]], axis=1)


def tap_norm(off):
    total = jnp.zeros_like(off)
    for k in range(-3, 5):
        u = (k - off) / 1.5
        total = total + jnp.exp(-u * u)
    return 1.0 / total


def taps(coord, cell, off, inv, ok=None):
    d = coord - cell
    u = (d - off) / 1.5
    hit = (d >= -3.0) & (d <= 4.0)
    if ok is not None:
        hit = hit & ok
    return jnp.where(hit, jnp.exp(-u * u) * inv, 0.0)


def row_coord(n, shift):
    return (lax.broadcasted_iota(jnp.int32, (n, 1), 0) + shift).astype(F32)


def cyc_coord(n, split):
    r = lax.broadcasted_iota(jnp.int32, (n, 1), 0)
    return jnp.where(r < split, r, r - n).astype(F32)


def pack_gy(info, vel, cells, offs, c_out, d_out, pts):
    ix, iy, px, py = place(info)
    cells, offs = use(cells), use(offs)
    for n in range(3):
        for h in range(2):
            pts[2 * n + h : 2 * n + h + 1, :] = cells[n, 0, :, 128 * h : 128 * h + 128].astype(F32)
            pts[6 + 2 * n + h : 7 + 2 * n + h, :] = offs[n, 0, :, 128 * h : 128 * h + 128]

    vel = use(vel)

    def body(t, u):
        c = t // W
        x = t - c * W
        to_hi = vel[c, x, W - 4 : W, :]
        to_lo = vel[c, x, 0:4, :]
        c_out[t] = jnp.where(py == 0, to_hi, to_lo)
        d_out[t] = jnp.where(py == 0, to_lo, to_hi)

    rows(0, 3 * W, 24, body)
    for k in range(3):
        c_out[3 * W + k] = pts[4 * k : 4 * k + 4, :]
        d_out[3 * W + k] = pts[4 * k : 4 * k + 4, :]


def pack_gx(info, vel, pts, c_in, d_in, a_out, b_out):
    ix, iy, px, py = place(info)
    ok_hi, ok_lo = okf(iy < NGY - 1), okf(iy > 0)
    off_a = jnp.where(px == 0, W - 4, 0)
    off_b = W - 4 - off_a
    for out, off in ((a_out, off_a), (b_out, off_b)):
        for c in range(3):
            for k in range(4):
                x = off + k
                e = c * 4 + k
                hi, lo = hi_lo(py, c_in[c * W + x], d_in[c * W + x])
                out[e, 0:W, :] = vel[c, x]
                out[e, W : W + 4, :] = hi * ok_hi
                out[e, W + 4 : W + 8, :] = lo * ok_lo
        out[12, 0:12, :] = pts[...]
        for k in range(3):
            hi, lo = hi_lo(py, c_in[3 * W + k], d_in[3 * W + k])
            out[12, 12 + 4 * k : 16 + 4 * k, :] = hi
            out[12, 24 + 4 * k : 28 + 4 * k, :] = lo
        out[12, 36:40, :] = jnp.zeros((4, 128), F32)


def force_kernel(
    info, vel, pts, drags, blades, c_in, d_in, a_in, b_in,
    g_out, f_out, own_out, c_out, d_out, cg_out, dg_out, pts9,
    wide, rv, vt, dom, tmp, tmp1,
):
    ix, iy, px, py = place(info)
    ok_hi, ok_lo = okf(iy < NGY - 1), okf(iy > 0)
    okx_hi, okx_lo = okf(ix < NGX - 1), okf(ix > 0)

    def fill(t, u):
        c = t // W
        x = t - c * W
        hi, lo = hi_lo(py, c_in[t], d_in[t])
        wide[c, x + 4, 0:W, :] = vel[c, x]
        wide[c, x + 4, W : W + 4, :] = hi * ok_hi
        wide[c, x + 4, W + 4 : W + 8, :] = lo * ok_lo

    rows(0, 3 * W, 24, fill)
    for c in range(3):
        for k in range(4):
            e = c * 4 + k
            hi, lo = hi_lo(px, a_in[e], b_in[e])
            wide[c, W + 4 + k] = hi * okx_hi
            wide[c, k] = lo * okx_lo

    start_x = (ix * W).astype(F32)
    start_y = (iy * W).astype(F32)
    cx = vec(pts, 0) - start_x
    cy = vec(pts, 2) - start_y
    cz = vec(pts, 4)
    ox, oy, oz = vec(pts, 6), vec(pts, 8), vec(pts, 10)
    nx, ny, nz = tap_norm(ox), tap_norm(oy), tap_norm(oz)
    z = row_coord(128, 0)

    wz = taps(z, cz, oz, nz)
    wz_hi, wz_lo = split3(wz)
    wz3 = jnp.concatenate([wz_hi, wz_lo, wz_hi], axis=0)
    wx40 = taps(row_coord(40, -4), cx, ox, nx)
    wy40 = taps(cyc_coord(40, 36), cy, oy, ny)
    acc = [None] * 3
    for t in range(5):
        for c in range(3):
            part = wide[c, t * 8 : t * 8 + 8].reshape(320, 128)
            hi, lo = split3(part)
            r = dot(jnp.concatenate([hi, hi, lo], axis=1), wz3).reshape(8, 40, P_)
            for k in range(8):
                m = r[k] * wx40[t * 8 + k : t * 8 + k + 1, :]
                acc[c] = m if acc[c] is None else acc[c] + m
    sampled = [jnp.sum(acc[c] * wy40, axis=0, keepdims=True) for c in range(3)]
    drag, blade = drags[0], blades[0]
    slot = lax.broadcasted_iota(jnp.int32, (1, P_), 1)
    live = okf(slot < info[2])
    speed = jnp.sqrt(sampled[0] * sampled[0] + sampled[1] * sampled[1] + sampled[2] * sampled[2] + blade * blade)
    pull = -(drag * speed * live)
    force = [pull * s for s in sampled]
    for c in range(3):
        f_out[2 * c : 2 * c + 1, :] = force[c][:, 0:128]
        f_out[2 * c + 1 : 2 * c + 2, :] = force[c][:, 128:256]
    f_out[6:8, :] = jnp.zeros((2, 128), F32)

    def axis_taps(coord, cell, off, inv, start, size):
        def at(shift):
            q = coord + shift
            ok = (q + start >= 0.0) & (q + start < size)
            return taps(q, cell, off, inv, ok)

        return at(0.0), at(1.0) - at(-1.0)

    wx, dx = axis_taps(row_coord(48, -5), cx, ox, nx, start_x, float(W * NGX))
    wy, dy = axis_taps(cyc_coord(48, 40), cy, oy, ny, start_y, float(W * NGY))
    wzz, dz = axis_taps(z, cz, oz, nz, 0.0, 128.0)
    r1_hi, r1_lo = split3(-0.5 * wzz.T)
    r2_hi, r2_lo = split3(-0.5 * dz.T)
    right = jnp.concatenate([r1_hi, r2_hi, r1_lo, r2_lo, r1_hi, r2_hi], axis=0)
    fy_dy = force[1] * dy
    fx_wy = force[0] * wy
    fz_wy = force[2] * wy

    dom[...] = y_domain(48, W, 8, iy * W, W * NGY)
    zm = z_masks(1)
    for x in range(W):
        vx = wide[0, x + 5, 0:W, :] - wide[0, x + 3, 0:W, :]
        vy = wide[1, x + 4]
        vy = pltpu.roll(vy, 39, 0)[0:W] - pltpu.roll(vy, 1, 0)[0:W]
        vz = wide[2, x + 4, 0:W, :]
        vz = pltpu.roll(vz, 127, 1) * zm[1] - pltpu.roll(vz, 1, 1) * zm[0]
        rv[x] = -0.5 * (vx + vy + vz)

    for t in range(6):
        l1, l2 = [], []
        for k in range(7):
            i = t * 7 + k
            row_w = wx[i : i + 1, :]
            row_d = dx[i : i + 1, :]
            l1.append(row_d * fx_wy + row_w * fy_dy)
            l2.append(row_w * fz_wy)
        l1_hi, l1_lo = split3(jnp.concatenate(l1, axis=0))
        l2_hi, l2_lo = split3(jnp.concatenate(l2, axis=0))
        left = jnp.concatenate([l1_hi, l2_hi, l1_hi, l2_hi, l1_lo, l2_lo], axis=1)
        r = dot(left, right).reshape(7, 48, 128)
        for k in range(7):
            i = t * 7 + k
            share = r[k] * (dom[...] * x_in(ix * W - 5, i, W * NGX))
            if 5 <= i < W + 5:
                g_out[i + 4, 0:W, :] = share[0:W] + rv[i - 5]
                g_out[i + 4, W:48, :] = share[W:48]
            else:
                g_out[i + 4] = share

    zero = jnp.zeros((48, 128), F32)
    for i in (0, 1, 2, 3, 46, 47, 48, 49):
        g_out[i] = zero
    vt[0] = zero
    vt[49] = zero
    double_sweep(vt, g_out, 1, 49, 1, dom, ix * W - 9, W * NGX)

    def emit(k, u, r):
        tmp1[k] = r

    restrict_rows(emit, vt, g_out, tmp, 0, 24, 1, 1, 24)
    even = (lanes((24, 128)) & 1) == 0
    for k in range(12):
        own = jnp.where(even, tmp1[2 * k], tmp1[2 * k + 1])
        own_out[k] = own
        to_hi = own[4:20]
        to_lo = jnp.concatenate([own[20:24], own[0:12]], axis=0)
        c_out[k] = jnp.where(py == 0, to_hi, to_lo)
        d_out[k] = jnp.where(py == 0, to_lo, to_hi)
    for out in (c_out, d_out):
        out[12, 0:8, :] = f_out[...]
        out[12, 8:16, :] = jnp.zeros((8, 128), F32)

    for i in range(42):
        to_hi = g_out[i + 4, 24:40, :]
        to_lo = jnp.concatenate([g_out[i + 4, 40:48, :], g_out[i + 4, 0:8, :]], axis=0)
        cg_out[i] = jnp.where(py == 0, to_hi, to_lo)
        dg_out[i] = jnp.where(py == 0, to_lo, to_hi)
    pts9[0, 0:12, :] = pts[...]
    for k in range(3):
        hi, lo = hi_lo(py, c_in[3 * W + k], d_in[3 * W + k])
        pts9[1, 4 * k : 4 * k + 4, :] = hi
        pts9[2, 4 * k : 4 * k + 4, :] = lo
    hi, lo = hi_lo(px, a_in[12], b_in[12])
    for m in range(3):
        pts9[3 + m, 0:12, :] = hi[12 * m : 12 * m + 12]
        pts9[6 + m, 0:12, :] = lo[12 * m : 12 * m + 12]
    for k in range(9):
        pts9[k, 12:16, :] = jnp.zeros((4, 128), F32)


def merge_g(info, g, c_in, d_in, h_out, a_out, b_out):
    ix, iy, px, py = place(info)
    ok_hi, ok_lo = okf(iy < NGY - 1), okf(iy > 0)

    def body(i, u):
        hi, lo = hi_lo(py, c_in[i], d_in[i])
        hi, lo = hi * ok_hi, lo * ok_lo
        v = g[i + 4]
        h_out[i, 0:8, :] = v[0:8] + lo[8:16]
        h_out[i, 8:24, :] = v[8:24]
        h_out[i, 24:40, :] = v[24:40] + hi
        h_out[i, 40:48, :] = v[40:48] + lo[0:8]

    rows(0, 42, 42, body)
    off_a = jnp.where(px == 0, 31, 0)
    off_b = 31 - off_a

    def pack(k, u):
        a_out[k] = h_out[off_a + k]
        b_out[k] = h_out[off_b + k]

    rows(0, 11, 11, pack)


def emit_level1(c_out, tmp1, v2, b, tmp):
    lane = lanes((16, 128))

    def emit(k, u, r):
        tmp1[k] = r

    restrict_rows(emit, v2, b, tmp, 0, 16, 6, 1, 16)
    for k in range(8):
        c_out[k] = jnp.where((lane & 1) == 0, tmp1[2 * k], tmp1[2 * k + 1])


def down0(info, h, a_in, b_in, b_out, dom):
    ix, iy, px, py = place(info)
    okx_hi, okx_lo = okf(ix < NGX - 1), okf(ix > 0)
    dom[...] = y_domain(48, W, 8, iy * W, W * NGY)
    start = ix * W - 6

    def inner(i, u):
        b_out[i] = h[i - 1] * dom[...] * x_in(start, i, W * NGX)

    rows(1, 43, 42, inner)
    zero = jnp.zeros((48, 128), F32)
    b_out[0] = zero
    b_out[43] = zero

    def rim(k, u):
        hi, lo = hi_lo(px, a_in[k], b_in[k])
        b_out[k] = b_out[k] + lo * dom[...] * (okx_lo * x_in(start, k, W * NGX))
        j = k + 33
        b_out[j] = b_out[j] + hi * dom[...] * (okx_hi * x_in(start, j, W * NGX))

    rows(0, 11, 11, rim)


def merge1_gx(info, own, f, c_in, d_in, s_out, a_out, b_out):
    ix, iy, px, py = place(info)
    ok_hi, ok_lo = okf(iy < NGY - 1), okf(iy > 0)
    for k in range(12):
        hi, lo = hi_lo(py, c_in[k], d_in[k])
        hi, lo = hi * ok_hi, lo * ok_lo
        s_out[k, 0:4, :] = own[k, 0:4, :] + lo[12:16]
        s_out[k, 4:12, :] = own[k, 4:12, :]
        s_out[k, 12:20, :] = own[k, 12:20, :] + hi[0:8]
        s_out[k, 20:28, :] = hi[8:16]
        s_out[k, 28:36, :] = jnp.zeros((8, 128), F32)
        s_out[k, 36:44, :] = lo[0:8]
        s_out[k, 44:48, :] = own[k, 20:24, :] + lo[8:12]
    off_a = jnp.where(px == 0, 5, 0)
    off_b = 5 - off_a
    hi, lo = hi_lo(py, c_in[12], d_in[12])
    for out, off in ((a_out, off_a), (b_out, off_b)):
        for k in range(7):
            out[k] = s_out[off + k]
        out[7, 0:8, :] = f[...]
        out[7, 8:16, :] = jnp.zeros((8, 128), F32)
        out[7, 16:32, :] = hi
        out[7, 32:48, :] = lo


def down1_shares(info, shares, f, c_in, d_in, a_in, b_in, pairs, packed, f9, s_b1, s_v1, s_b2, s_v2, dom1, dom2, tmp, tmp3):
    ix, iy, px, py = place(info)
    okx_hi, okx_lo = okf(ix < NGX - 1), okf(ix > 0)
    dom1[...] = y_domain(48, 16, 16, iy * 16, W * NGY // 2)
    start1, n1x = ix * 16 - 10, W * NGX // 2
    for p in range(18):
        total = None
        if 3 <= p < 15:
            total = shares[p - 3]
        if p < 7:
            part = hi_lo(px, a_in[p], b_in[p])[1] * okx_lo
            total = part if total is None else total + part
        if p >= 11:
            part = hi_lo(px, a_in[p - 11], b_in[p - 11])[0] * okx_hi
            total = part if total is None else total + part
        pairs[p] = total * (dom1[...] * x_in(start1, 2 * p, n1x))
    levels_down(info, pairs, s_b1, s_v1, s_b2, s_v2, dom1, dom2, tmp)
    pack3(packed, s_b2, s_v2, tmp, tmp3)
    fhi, flo = hi_lo(py, c_in[12, 0:8, :], d_in[12, 0:8, :])
    f9[0] = f[...]
    f9[1] = fhi
    f9[2] = flo
    hi, lo = hi_lo(px, a_in[7], b_in[7])
    for m in range(3):
        f9[3 + m] = hi[16 * m : 16 * m + 8]
        f9[6 + m] = lo[16 * m : 16 * m + 8]


def pack1_gx(info, own, c_in, d_in, a_out, b_out):
    ix, iy, px, py = place(info)
    ok_hi, ok_lo = okf(iy < NGY - 1), okf(iy > 0)
    off_a = jnp.where(px == 0, 3, 0)
    off_b = 3 - off_a
    for out, off in ((a_out, off_a), (b_out, off_b)):
        for k in range(5):
            hi, lo = hi_lo(py, c_in[off + k], d_in[off + k])
            out[k, 0:16, :] = own[off + k]
            out[k, 16:32, :] = hi * ok_hi
            out[k, 32:48, :] = lo * ok_lo


def down1(info, own, c_in, d_in, a_in, b_in, pairs, packed, s_b1, s_v1, s_b2, s_v2, dom1, dom2, tmp, tmp3):
    ix, iy, px, py = place(info)
    ok_hi, ok_lo = okf(iy < NGY - 1), okf(iy > 0)
    okx_hi, okx_lo = okf(ix < NGX - 1), okf(ix > 0)
    for k in range(8):
        hi, lo = hi_lo(py, c_in[k], d_in[k])
        pairs[5 + k, 0:16, :] = own[k]
        pairs[5 + k, 16:32, :] = hi * ok_hi
        pairs[5 + k, 32:48, :] = lo * ok_lo
    for k in range(5):
        hi, lo = hi_lo(px, a_in[k], b_in[k])
        pairs[k] = lo * okx_lo
        pairs[13 + k] = hi * okx_hi
    levels_down(info, pairs, s_b1, s_v1, s_b2, s_v2, dom1, dom2, tmp)
    pack3(packed, s_b2, s_v2, tmp, tmp3)


def levels_down(info, pairs, b1, v1, b2, v2, dom1, dom2, tmp):
    ix, iy, px, py = place(info)
    n1x, n1y = W * NGX // 2, W * NGY // 2
    dom1[...] = y_domain(48, 16, 16, iy * 16, n1y)
    dom2[...] = y_domain(24, 8, 8, iy * 8, n1y // 2)
    even = (lanes((48, 128)) & 1) == 0
    for k in range(18):
        p = pairs[k]
        b1[2 * k] = jnp.where(even, p, pltpu.roll(p, 1, 1))
        b1[2 * k + 1] = jnp.where(even, pltpu.roll(p, 127, 1), p)
    zero1 = jnp.zeros((48, 128), F32)
    v1[0] = zero1
    v1[35] = zero1
    start1 = ix * 16 - 10
    double_sweep(v1, b1, 1, 35, 2, dom1, start1, n1x)
    start2 = ix * 8 - 4

    def emit2(k, u, r):
        b2[k] = r * dom2[...] * x_in(start2, k, n1x // 2)

    restrict_rows(emit2, v1, b1, tmp, 0, 16, 2, 2, 24)
    zero2 = jnp.zeros((24, 128), F32)
    v2[0] = zero2
    v2[15] = zero2
    double_sweep(v2, b2, 1, 15, 4, dom2, start2, n1x // 2)


def pack3(packed, b2, v2, tmp, tmp3):
    def emit3(k, u, r):
        tmp3[k] = r

    restrict_rows(emit3, v2, b2, tmp, 0, 4, 4, 4, 8)
    row = lax.broadcasted_iota(jnp.int32, (8, 128), 0)
    lane = lanes((8, 128)) & 7
    first = okf((lane == row) & (row < 4))
    second = okf((lane == row + 4) & (row < 4))
    for q in range(2):
        s = tmp3[2 * q] * first + tmp3[2 * q + 1] * second
        packed[q : q + 1, :] = jnp.sum(s, axis=0, keepdims=True)


def coarse_up(info, g, pairs, s):
    ix, iy, px, py = place(info)
    n3x = NGX * 4

    def load(d, u):
        at = ix - 7 + d
        ok = okf((at >= 0) & (at < NGX))
        at = jnp.clip(at, 0, NGX - 1)
        base = d * 16
        s.px[pl.ds(pl.multiple_of(base, 8), 8), :] = g[at, pl.ds(0, 8, stride=2), :] * ok
        s.px[pl.ds(pl.multiple_of(base + 8, 8), 8), :] = g[at, pl.ds(1, 8, stride=2), :] * ok

    rows(0, 15, 15, load)
    src = lax.broadcasted_iota(jnp.int32, (128, 1024), 0)
    dst = lax.broadcasted_iota(jnp.int32, (128, 1024), 1)
    pick = okf(src == ((dst & 127) >> 3) * 8 + (dst >> 7)).astype(BF16)
    x = s.px[...]
    x_hi, x_lo = split3(x)
    x_lo2 = (x - x_hi.astype(F32) - x_lo.astype(F32)).astype(BF16)
    s.pu[...] = dot(x_hi, pick) + dot(x_lo, pick) + dot(x_lo2, pick)

    def place3(d, u):
        for q in range(2):
            for j in range(8):
                part = s.pu[pl.ds(pl.multiple_of(d * 16 + q * 8, 8), 8), j * 128 : (j + 1) * 128]
                s.b3[d * 4 + 2 * q + (j >> 2), pl.ds(j & 3, 8, stride=4), :] = part

    rows(0, 15, 15, place3)
    e3, e4, e5 = y_edge(32), y_edge(16), y_edge(8)
    start3, start4, start5 = (ix - 7) * 4, (ix - 7) * 2, ix - 7
    z3, z4, z5 = jnp.zeros((32, 128), F32), jnp.zeros((16, 128), F32), jnp.zeros((8, 128), F32)
    for r, z, n in ((s.v3, z3, 60), (s.b4, z4, 30), (s.v4, z4, 30), (s.b5, z5, 15), (s.v5, z5, 15), (s.w5, z5, 15)):
        r[0] = z
        r[n - 1] = z
    double_sweep(s.v3, s.b3, 1, 59, 8, None, start3, n3x, e3)

    def emit4(k, u, r):
        s.b4[k] = r * x_in(start4, k, n3x // 2)

    restrict_rows(emit4, s.v3, s.b3, s.tmp, 1, 29, 0, 8, 16, e3)
    double_sweep(s.v4, s.b4, 1, 29, 16, None, start4, n3x // 2, e4)

    def emit5(k, u, r):
        s.b5[k] = r * x_in(start5, k, NGX)

    restrict_rows(emit5, s.v4, s.b4, s.tmp, 1, 14, 0, 16, 8, e4)
    double_sweep(s.v5, s.b5, 1, 14, 32, None, start5, NGX, e5)
    sweep(s.w5, s.v5, s.b5, 1, 14, 32, None, start5, NGX, e5)
    sweep(s.v5, s.w5, s.b5, 1, 14, 32, None, start5, NGX, e5)

    correct(s.w4, s.v4, s.v5, s.tmp, 5, 10, 0, ((0, 8, 0),), 16, None, start4, n3x // 2)
    sweep(s.v4, s.w4, s.b4, 11, 19, 16, None, start4, n3x // 2, e4)
    correct(s.w3, s.v3, s.v4, s.tmp, 12, 18, 0, ((0, 16, 0),), 32, None, start3, n3x)
    sweep(s.v3, s.w3, s.b3, 26, 34, 8, None, start3, n3x, e3)

    levels_down(info, use(pairs), s.b1, s.v1, s.b2, s.v2, s.dom1, s.dom2, s.tmp)
    turn = lax.rem(32 - 4 * iy, 32)

    def shifted(k):
        return pltpu.roll(s.v3[k + 26], turn, 0)

    start2, start1 = ix * 8 - 4, ix * 16 - 10
    n2x, n1x = n3x * 2, n3x * 4
    correct(s.w2, s.v2, None, s.tmp, 0, 8, 0, ((0, 8, 0), (28, 4, 16)), 24, s.dom2, start2, n2x, shifted)
    sweep(s.e2, s.w2, s.b2, 2, 14, 4, s.dom2, start2, n2x)
    correct(s.w1, s.v1, s.e2, s.tmp, 2, 14, 2, ((0, 24, 0),), 48, s.dom1, start1, n1x)
    sweep(s.e1, s.w1, s.b1, 7, 29, 2, s.dom1, start1, n1x)


class Bag:
    pass


COARSE = (
    ("px", (240, 128)),
    ("pu", (240, 1024)),
    ("b3", (60, 32, 128)),
    ("v3", (60, 32, 128)),
    ("w3", (60, 32, 128)),
    ("b4", (30, 16, 128)),
    ("v4", (30, 16, 128)),
    ("w4", (30, 16, 128)),
    ("b5", (15, 8, 128)),
    ("v5", (15, 8, 128)),
    ("w5", (15, 8, 128)),
    ("w2", (16, 24, 128)),
    ("e2", (16, 24, 128)),
    ("w1", (36, 48, 128)),
    ("e1", (36, 48, 128)),
    ("w0", (44, 48, 128)),
    ("x0", (44, 48, 128)),
    ("dom0", (48, 128)),
    ("dom1", (48, 128)),
    ("dom2", (24, 128)),
    ("b1", (36, 48, 128)),
    ("v1", (36, 48, 128)),
    ("b2", (16, 24, 128)),
    ("v2", (16, 24, 128)),
    ("v0", (44, 48, 128)),
    ("tmp", (32, 48, 128)),
    ("tmp1", (16, 16, 128)),
)
COARSE_SCRATCH = [pltpu.VMEM(shape, F32) for name, shape in COARSE]


def bag(refs):
    s = Bag()
    for (name, shape), ref in zip(COARSE, refs):
        setattr(s, name, ref)
    return s


PIECES0 = ((0, 20, 0), (44, 4, 40))


def middle(info, g, b0, pairs, v_late, c_out, *scratch):
    s = bag(scratch)
    ix, iy, px, py = place(info)
    coarse_up(info, g, pairs, s)
    s.dom0[...] = y_domain(48, W, 8, iy * W, W * NGY)
    start, size = ix * W - 6, W * NGX
    b0 = use(b0)
    zero = jnp.zeros((48, 128), F32)
    s.v0[0] = zero
    s.v0[43] = zero
    double_sweep(s.v0, b0, 1, 43, 1, s.dom0, start, size)
    correct(s.w0, s.v0, s.e1, s.tmp, 7, 29, -14, PIECES0, 48, s.dom0, start, size)
    sweep(s.x0, s.w0, b0, 2, 42, 1, s.dom0, start, size)
    sweep(s.w0, s.x0, b0, 3, 41, 1, s.dom0, start, size)
    v_out = v_late.ref
    sweep(v_out, s.w0, b0, 4, 40, 1, s.dom0, start, size)
    for i in (0, 1, 2, 3, 40, 41, 42, 43):
        v_out[i] = zero
    v_late.flush()
    emit_level1(c_out, s.tmp1, v_out, b0, s.tmp)


def final(info, g, b0, v0, pairs, pushed, vel_out, p_out, *scratch):
    s = bag(scratch)
    ix, iy, px, py = place(info)
    coarse_up(info, g, pairs, s)
    s.dom0[...] = y_domain(48, W, 8, iy * W, W * NGY)
    start, size = ix * W - 6, W * NGX
    b0, v0 = use(b0), use(v0)
    correct(s.w0, v0, s.e1, s.tmp, 9, 27, -14, PIECES0, 48, s.dom0, start, size)
    sweep(s.x0, s.w0, b0, 5, 39, 1, s.dom0, start, size)
    zm = z_masks(1)
    pushed = use(pushed)

    def body(x, u):
        p = s.x0[x + 6]
        own = p[0:W]
        p_out[x] = own
        gx = s.x0[x + 7, 0:W, :] - s.x0[x + 5, 0:W, :]
        gy = pltpu.roll(p, 47, 0)[0:W] - pltpu.roll(p, 1, 0)[0:W]
        gz = pltpu.roll(own, 127, 1) * zm[1] - pltpu.roll(own, 1, 1) * zm[0]
        vel_out[0, x] = pushed[0, x] - 0.5 * gx
        vel_out[1, x] = pushed[1, x] - 0.5 * gy
        vel_out[2, x] = pushed[2, x] - 0.5 * gz

    rows(0, W, 32, body)


def push_kernel(info, vel, pts9, f9, out):
    ix, iy, px, py = place(info)
    ok = {-1: (okf(ix > 0), okf(iy > 0)), 0: (1.0, 1.0), 1: (okf(ix < NGX - 1), okf(iy < NGY - 1))}
    start_x = (ix * W).astype(F32)
    start_y = (iy * W).astype(F32)
    order = ((0, 0), (0, 1), (0, -1), (1, 0), (1, 1), (1, -1), (-1, 0), (-1, 1), (-1, -1))
    for slot, (ox_, oy_) in enumerate(order):
        q, fq = pts9.at[slot], f9.at[slot]
        cx, cy, cz = vec(q, 0) - start_x, vec(q, 2) - start_y, vec(q, 4)
        ox, oy, oz = vec(q, 6), vec(q, 8), vec(q, 10)
        keep = ok[ox_][0] * ok[oy_][1]
        force = [vec(fq, 2 * c) * keep for c in range(3)]
        wx = taps(row_coord(32, 0), cx, ox, tap_norm(ox))
        y0, yn = {0: (0, 32), 1: (24, 8), -1: (0, 8)}[oy_]
        wy = taps(row_coord(yn, y0), cy, oy, tap_norm(oy))
        wz = taps(row_coord(128, 0), cz, oz, tap_norm(oz)).T
        r_hi, r_lo = split3(wz)
        right = jnp.concatenate([r_hi, r_lo, r_hi], axis=0)
        fy = [force[c] * wy for c in range(3)]
        x0, xn = {0: (0, 32), 1: (28, 4), -1: (0, 4)}[ox_]
        step = min(xn, 4 if oy_ == 0 else 16)

        def spread(t, x0=x0, step=step, fy=fy, right=right, y0=y0, yn=yn, slot=slot, wx=wx):
            at = x0 + t * step
            left = []
            for k in range(step):
                row = wx[at + k : at + k + 1, :]
                left += [row * fy[c] for c in range(3)]
            hi, lo = split3(jnp.concatenate(left, axis=0))
            r = dot(jnp.concatenate([hi, hi, lo], axis=1), right).reshape(step, 3, yn, 128)
            for k in range(step):
                for c in range(3):
                    base = vel if slot == 0 else out
                    out[c, at + k, y0 : y0 + yn, :] = base[c, at + k, y0 : y0 + yn, :] + r[k, c]

        for t in range(xn // step):
            spread(t)


def gather3(packed):
    everyone = jnp.broadcast_to(packed[None], (NGX * NGY, 2, 128))
    return lax.all_to_all(everyone, AXES, 0, 0, tiled=True).reshape(NGX, 16, 128)


LEVELS12 = [(18, 48, 128), (2, 128)]
DOWN1 = [
    VMEM((36, 48, 128), F32), VMEM((36, 48, 128), F32), VMEM((16, 24, 128), F32), VMEM((16, 24, 128), F32),
    VMEM((48, 128), F32), VMEM((24, 128), F32), VMEM((32, 48, 128), F32), VMEM((4, 8, 128), F32),
]


def per_device(velocity, point_cells, point_offsets, point_count, drag, blade_speed):
    info = jnp.stack([lax.axis_index("gx"), lax.axis_index("gy"), point_count.reshape(())]).astype(jnp.int32)

    c0, d0, pts = call(
        pack_gy, [(99, 4, 128)] * 2 + [(12, 128)], [], info, velocity, point_cells, point_offsets
    )
    c0, d0 = swap_gy(c0, d0)
    a0, b0 = call(pack_gx, [(13, 40, 128)] * 2, [], info, velocity, pts, c0, d0)
    a0, b0 = swap_gx(a0, b0)
    g, f, own1, c1, d1, cg, dg, pts9 = call(
        force_kernel,
        [(50, 48, 128), (8, 128), (12, 24, 128), (13, 16, 128), (13, 16, 128), (42, 16, 128), (42, 16, 128), (9, 16, 128)],
        [
            VMEM((3, 40, 40, 128), F32), VMEM((W, W, 128), F32), VMEM((50, 48, 128), F32), VMEM((48, 128), F32),
            VMEM((32, 48, 128), F32), VMEM((24, 24, 128), F32),
        ],
        info, velocity, pts, drag, blade_speed, c0, d0, a0, b0,
    )
    c1, d1 = swap_gy(c1, d1)
    shares, a1, b1 = call(merge1_gx, [(12, 48, 128), (8, 48, 128), (8, 48, 128)], [], info, own1, f, c1, d1)
    a1, b1 = swap_gx(a1, b1)
    pairs, packed, f9 = call(down1_shares, LEVELS12 + [(9, 8, 128)], DOWN1, info, shares, f, c1, d1, a1, b1)
    packed, g, cg, dg = lax.optimization_barrier((packed, g, cg, dg))
    gathered = gather3(packed)
    cg, dg = swap_gy(cg, dg)
    h, ag, bg = call(merge_g, [(42, 48, 128), (11, 48, 128), (11, 48, 128)], [], info, g, cg, dg)
    ag, bg = swap_gx(ag, bg)
    (rhs,) = call(down0, [(44, 48, 128)], [VMEM((48, 128), F32)], info, h, ag, bg)
    v0, own1 = call(
        middle, [(44, 48, 128), (8, 16, 128)], COARSE_SCRATCH, info, gathered, rhs, pairs, late=(2, 3), early=(0,)
    )
    c1, d1 = swap_gy(own1, own1)
    a1, b1 = call(pack1_gx, [(5, 48, 128)] * 2, [], info, own1, c1, d1)
    a1, b1 = swap_gx(a1, b1)
    pairs, packed = call(down1, LEVELS12, DOWN1, info, own1, c1, d1, a1, b1)
    packed, pts9 = lax.optimization_barrier((packed, pts9))
    gathered = gather3(packed)
    (pushed,) = call(push_kernel, [(3, W, W, 128)], [], info, velocity, pts9, f9)
    vel_out, p_out = call(
        final, [(3, W, W, 128), (W, W, 128)], COARSE_SCRATCH, info, gathered, rhs, v0, pairs, pushed, late=(2, 3, 4, 5)
    )
    return vel_out, p_out


def solution(mesh):
    placed = (
        P(None, "gx", "gy", None),
        P(None, "gx", "gy", None),
        P(None, "gx", "gy", None),
        P("gx", "gy"),
        P("gx", "gy", None),
        P("gx", "gy", None),
    )
    return jax.shard_map(
        per_device,
        mesh=mesh,
        in_specs=placed,
        out_specs=(P(None, "gx", "gy", None), P("gx", "gy", None)),
        check_vma=False,
    )
```

```python
import functools

import jax
import jax.numpy as jnp
from jax import lax
from jax.experimental import pallas as pl
from jax.experimental.pallas import tpu as pltpu
from jax.sharding import PartitionSpec as P

AXES = ("gx", "gy")
NGX, NGY = 32, 8
W = 32
P_ = 256
F32 = jnp.float32
BF16 = jnp.bfloat16
VMEM = pltpu.VMEM
LIMIT = 24 * 1024 * 1024
WHOLE = 60 * 1024 * 1024


def swap(x, fx, fy):
    perm = [(i * NGY + j, fx(i) * NGY + fy(j)) for i in range(NGX) for j in range(NGY)]
    return lax.ppermute(x, AXES, perm)


def same(i):
    return i


def pair(i):
    return i ^ 1


def other(n):
    return lambda i: (i + 1) % n if i % 2 else (i - 1) % n


def swap_gx(a, b):
    return swap(a, pair, same), swap(b, other(NGX), same)


def swap_gy(c, d):
    return swap(c, same, pair), swap(d, same, other(NGY))


class Late:
    def __init__(self, copy, ref):
        self.copy, self.ref, self.done = copy, ref, False

    def get(self):
        if not self.done:
            self.copy.wait()
            self.done = True
        return self.ref


def use(x):
    return x.get() if isinstance(x, Late) else x


class Early:
    def __init__(self, copy, ref):
        self.copy, self.ref, self.sent = copy, ref, False

    def flush(self):
        if not self.sent:
            self.copy.start()
            self.sent = True


def call(kernel, out_shapes, scratch, *args, late=(), early=(), direct=()):
    nbytes = sum(a.size * 4 for a in args) + sum(4 * functools.reduce(lambda x, y: x * y, s) for s in out_shapes)
    n_in, n_out = len(args), len(out_shapes)

    def body(*refs):
        ins, outs = list(refs[:n_in]), list(refs[n_in : n_in + n_out])
        rest = refs[n_in + n_out :]
        own, rest = rest[: len(scratch)], rest[len(scratch) :]
        if late or early:
            bufs, sems = rest[:-1], rest[-1]
        for n, at in enumerate(late):
            copy = pltpu.make_async_copy(ins[at], bufs[n], sems.at[n])
            copy.start()
            ins[at] = Late(copy, bufs[n])
        for n, at in enumerate(early):
            k = len(late) + n
            outs[at] = Early(pltpu.make_async_copy(bufs[k], outs[at], sems.at[k]), bufs[k])
        kernel(*ins, *outs, *own)
        for at in late:
            use(ins[at])
        for at in early:
            outs[at].flush()
        for at in early:
            outs[at].copy.wait()

    specs = [pl.BlockSpec(memory_space=pltpu.SMEM)] + [
        pl.BlockSpec(memory_space=pltpu.HBM if n in late else VMEM) for n in range(1, n_in)
    ]
    extra = [VMEM(args[n].shape, args[n].dtype) for n in late] + [VMEM(out_shapes[n], F32) for n in early]
    if extra:
        extra.append(pltpu.SemaphoreType.DMA((len(extra),)))
    return pl.pallas_call(
        body,
        out_shape=[jax.ShapeDtypeStruct(s, F32) for s in out_shapes],
        in_specs=specs,
        out_specs=[pl.BlockSpec(memory_space=pltpu.HBM if n in early or n in direct else VMEM) for n in range(n_out)],
        scratch_shapes=list(scratch) + extra,
        compiler_params=pltpu.CompilerParams(vmem_limit_bytes=WHOLE if late else LIMIT),
        cost_estimate=pl.CostEstimate(flops=10_000_000, bytes_accessed=nbytes, transcendentals=0),
    )(*args)


def rows(lo, hi, unroll, body):
    n = hi - lo
    main = n // unroll if unroll < n else 0
    if main > 1:

        def step(t, c):
            for u in range(unroll):
                body(lo + t * unroll + u, u)
            return c

        lax.fori_loop(0, main, step, 0)
        lo = lo + main * unroll
    for i in range(lo, hi):
        body(i, i - lo)


def place(info):
    ix, iy = info[0], info[1]
    return ix, iy, ix % 2, iy % 2


def okf(cond):
    return jnp.where(cond, 1.0, 0.0).astype(F32)


def hi_lo(par, a, b):
    return jnp.where(par == 0, a, b), jnp.where(par == 0, b, a)


def lanes(shape=(1, 128)):
    return lax.broadcasted_iota(jnp.int32, shape, len(shape) - 1)


def z_masks(s):
    lane = lanes()
    return okf(lane >= s), okf(lane < 128 - s)


def neighbours(ref, i, v, s, zm, ym=None):
    size = v.shape[0]
    up = pltpu.roll(v, 1, 0)
    down = pltpu.roll(v, size - 1, 0)
    if ym is not None:
        up, down = up * ym[0], down * ym[1]
    low = pltpu.roll(v, s, 1) * zm[0]
    high = pltpu.roll(v, 128 - s, 1) * zm[1]
    return (ref[i - 1] + ref[i + 1]) + (up + down) + (low + high)


def x_in(start, i, size):
    g = start + i
    return okf((g >= 0) & (g < size))


def y_edge(size):
    r = lax.broadcasted_iota(jnp.int32, (size, 1), 0)
    return okf(r > 0), okf(r < size - 1)


def y_domain(size, own, hi, start, total):
    r = lax.broadcasted_iota(jnp.int32, (size, 128), 0)
    g = start + jnp.where(r < own + hi, r, r - size)
    return okf((g >= 0) & (g < total))


def double_sweep(dst, b, lo, hi, s, dom, start, size, ym=None, unroll=64):
    zm = z_masks(s)

    def body(i, u):
        v = b[i]
        c = x_in(start, i, size) * (1.0 / 49.0)
        out = (8.0 * v + neighbours(b, i, v, s, zm, ym)) * c
        if dom is not None:
            out = out * dom[...]
        dst[i] = out

    rows(lo, hi, unroll, body)


def sweep(dst, v_ref, b, lo, hi, s, dom, start, size, ym=None, unroll=64):
    zm = z_masks(s)

    def body(i, u):
        v = v_ref[i]
        c = x_in(start, i, size) * (1.0 / 7.0)
        out = (v + b[i] + neighbours(v_ref, i, v, s, zm, ym)) * c
        if dom is not None:
            out = out * dom[...]
        dst[i] = out

    rows(lo, hi, unroll, body)


def z_pairs(t, s):
    lane = lanes(t.shape)
    return t + jnp.where((lane & s) == 0, pltpu.roll(t, 128 - s, 1), pltpu.roll(t, s, 1))


def restrict_rows(emit, v_ref, b, tmp, klo, khi, base, s, keep, ym=None, unroll=64):
    zm = z_masks(s)

    def first(k, u):
        i = base + 2 * k
        total = None
        for d in range(2):
            v = v_ref[i + d]
            r = b[i + d] - 6.0 * v + neighbours(v_ref, i + d, v, s, zm, ym)
            total = r if total is None else total + r
        tmp[u, 0 : total.shape[0], :] = total

    def second(k, u):
        both = tmp[u, pl.ds(0, keep, stride=2), :] + tmp[u, pl.ds(1, keep, stride=2), :]
        emit(k, u, z_pairs(both, s) * 0.5)

    rows(klo, khi, unroll, first)
    rows(klo, khi, unroll, second)


def correct(dst, v_ref, e_ref, tmp, klo, khi, base, pieces, size, dom, start, total, get=None, unroll=64):
    def first(k, u):
        e = e_ref[k] if get is None else get(k)
        for at, count, to in pieces:
            part = e[at : at + count]
            tmp[u, pl.ds(to, count, stride=2), :] = part
            tmp[u, pl.ds(to + 1, count, stride=2), :] = part

    def second(k, u):
        wide = tmp[u, 0:size, :]
        for d in range(2):
            i = base + 2 * k + d
            out = v_ref[i] + wide
            if dom is not None:
                out = out * dom[...]
            dst[i] = out * x_in(start, i, total)

    rows(klo, khi, unroll, first)
    rows(klo, khi, unroll, second)


def split3(x):
    hi = x.astype(BF16)
    lo = (x - hi.astype(F32)).astype(BF16)
    return hi, lo


def dot(a, b):
    return jnp.dot(a, b, preferred_element_type=F32)


def vec(ref, at):
    return jnp.concatenate([ref[at : at + 1, :], ref[at + 1 : at + 2, :]], axis=1)


def tap_norm(off):
    total = jnp.zeros_like(off)
    for k in range(-3, 5):
        u = (k - off) / 1.5
        total = total + jnp.exp(-u * u)
    return 1.0 / total


def taps(coord, cell, off, inv, ok=None):
    d = coord - cell
    u = (d - off) / 1.5
    hit = (d >= -3.0) & (d <= 4.0)
    if ok is not None:
        hit = hit & ok
    return jnp.where(hit, jnp.exp(-u * u) * inv, 0.0)


def row_coord(n, shift):
    return (lax.broadcasted_iota(jnp.int32, (n, 1), 0) + shift).astype(F32)


def cyc_coord(n, split):
    r = lax.broadcasted_iota(jnp.int32, (n, 1), 0)
    return jnp.where(r < split, r, r - n).astype(F32)


def pack_gx(info, low, high, c_in, d_in, a_out, b_out):
    ix, iy, px, py = place(info)
    ok_hi, ok_lo = okf(iy < NGY - 1), okf(iy > 0)
    off_a = jnp.where(px == 0, W - 4, 0)
    off_b = W - 4 - off_a
    for out, off in ((a_out, off_a), (b_out, off_b)):
        for c in range(3):
            for k in range(4):
                x = off + k
                e = c * 4 + k
                hi, lo = hi_lo(py, c_in[c * W + x], d_in[c * W + x])
                out[e, 0:W, :] = jnp.where(off > 0, high[c, k], low[c, k])
                out[e, W : W + 4, :] = hi * ok_hi
                out[e, W + 4 : W + 8, :] = lo * ok_lo


def points(info, cells, offs):
    where = [cells[n, 0].astype(F32) for n in range(3)]
    local = [where[0] - (info[0] * W).astype(F32), where[1] - (info[1] * W).astype(F32), where[2]]
    off = [offs[n, 0] for n in range(3)]
    return where, local, off, [tap_norm(o) for o in off]


def sampled_lines(slabs, wx, first, wz3, acc):
    for c in range(3):
        n = slabs[c].shape[0]
        hi, lo = split3(slabs[c].reshape(40 * n, 128))
        r = dot(jnp.concatenate([hi, hi, lo], axis=1), wz3).reshape(n, 40, P_)
        for k in range(n):
            m = r[k] * wx[first + k : first + k + 1, :]
            acc[c] = m if acc[c] is None else acc[c] + m


def z_table(local, off, inv):
    hi, lo = split3(taps(row_coord(128, 0), local[2], off[2], inv[2]))
    return jnp.concatenate([hi, lo, hi], axis=0)


def sample_kernel(info, vel, cells, offs, c_in, d_in, part, xt, yt, zt):
    ix, iy, px, py = place(info)
    ok_hi, ok_lo = okf(iy < NGY - 1), okf(iy > 0)
    where, local, off, inv = points(info, cells, offs)
    wz3 = z_table(local, off, inv)
    wx = taps(row_coord(W, 0), local[0], off[0], inv[0])
    acc = [None] * 3
    for t in range(4):
        slabs = []
        for c in range(3):
            lines = []
            for x in range(t * 8, t * 8 + 8):
                hi, lo = hi_lo(py, c_in[c * W + x], d_in[c * W + x])
                lines.append(jnp.concatenate([vel[c, x], hi * ok_hi, lo * ok_lo], axis=0))
            slabs.append(jnp.stack(lines))
        sampled_lines(slabs, wx, t * 8, wz3, acc)
    for c in range(3):
        part[c] = acc[c]

    def axis_taps(d, coord, start, size):
        def at(shift):
            q = coord + shift
            ok = (q + start >= 0.0) & (q + start < size)
            return taps(q, local[d], off[d], inv[d], ok)

        return at(0.0), at(1.0) - at(-1.0)

    xt[0], xt[1] = axis_taps(0, row_coord(48, -5), (ix * W).astype(F32), float(W * NGX))
    yt[0], yt[1] = axis_taps(1, cyc_coord(48, 40), (iy * W).astype(F32), float(W * NGY))
    wz, dz = axis_taps(2, row_coord(128, 0), 0.0, 128.0)
    zt[0] = -0.5 * wz.T
    zt[1] = -0.5 * dz.T


def force_kernel(
    info, vel, cells, offs, drags, blades, part, xt, yt, zt, c_in, d_in, a_in, b_in,
    g_out, f_out, own_out, c_out, d_out,
    wide, rv, vt, dom, tmp, tmp1,
):
    ix, iy, px, py = place(info)
    ok_hi, ok_lo = okf(iy < NGY - 1), okf(iy > 0)
    okx_hi, okx_lo = okf(ix < NGX - 1), okf(ix > 0)

    def fill(t, u):
        c = t // W
        x = t - c * W
        hi, lo = hi_lo(py, c_in[t], d_in[t])
        wide[c, x + 4, 0:W, :] = vel[c, x]
        wide[c, x + 4, W : W + 4, :] = hi * ok_hi
        wide[c, x + 4, W + 4 : W + 8, :] = lo * ok_lo

    rows(0, 3 * W, 24, fill)
    for c in range(3):
        for k in range(4):
            e = c * 4 + k
            hi, lo = hi_lo(px, a_in[e], b_in[e])
            wide[c, W + 4 + k] = hi * okx_hi
            wide[c, k] = lo * okx_lo

    start_x = (ix * W).astype(F32)
    start_y = (iy * W).astype(F32)
    place_of, local, off, inv = points(info, cells, offs)
    (cx, cy, cz), (ox, oy, oz), (nx, ny, nz) = local, off, inv
    z = row_coord(128, 0)

    wz3 = z_table(local, off, inv)
    rim = row_coord(8, 0)
    wx8 = taps(jnp.where(rim < 4.0, rim - 4.0, rim + (W - 4.0)), cx, ox, nx)
    wy40 = taps(cyc_coord(40, 36), cy, oy, ny)
    acc = [part[c] for c in range(3)]
    slabs = [jnp.concatenate([wide[c, 0:4], wide[c, W + 4 : W + 8]], axis=0) for c in range(3)]
    sampled_lines(slabs, wx8, 0, wz3, acc)
    sampled = [jnp.sum(acc[c] * wy40, axis=0, keepdims=True) for c in range(3)]
    drag, blade = drags[0], blades[0]
    slot = lax.broadcasted_iota(jnp.int32, (1, P_), 1)
    live = okf(slot < info[2])
    speed = jnp.sqrt(sampled[0] * sampled[0] + sampled[1] * sampled[1] + sampled[2] * sampled[2] + blade * blade)
    pull = -(drag * speed * live)
    force = [pull * s for s in sampled]
    for n, q in enumerate(force + place_of + [ox, oy, oz]):
        f_out[2 * n : 2 * n + 1, :] = q[:, 0:128]
        f_out[2 * n + 1 : 2 * n + 2, :] = q[:, 128:256]
    f_out[18:32, :] = jnp.zeros((14, 128), F32)

    wx, dx, wy, dy = xt[0], xt[1], yt[0], yt[1]
    r1_hi, r1_lo = split3(zt[0])
    r2_hi, r2_lo = split3(zt[1])
    right_hi = jnp.concatenate([r1_hi, r2_hi], axis=0)
    right = jnp.concatenate([right_hi, jnp.concatenate([r1_lo, r2_lo], axis=0)], axis=1)
    fy_dy = force[1] * dy
    fx_wy = force[0] * wy
    fz_wy = force[2] * wy

    dom[...] = y_domain(48, W, 8, iy * W, W * NGY)
    zm = z_masks(1)
    for x in range(W):
        vx = wide[0, x + 5, 0:W, :] - wide[0, x + 3, 0:W, :]
        vy = wide[1, x + 4]
        vy = pltpu.roll(vy, 39, 0)[0:W] - pltpu.roll(vy, 1, 0)[0:W]
        vz = wide[2, x + 4, 0:W, :]
        vz = pltpu.roll(vz, 127, 1) * zm[1] - pltpu.roll(vz, 1, 1) * zm[0]
        rv[x] = -0.5 * (vx + vy + vz)

    for t in range(6):
        l1, l2 = [], []
        for k in range(7):
            i = t * 7 + k
            row_w = wx[i : i + 1, :]
            row_d = dx[i : i + 1, :]
            l1.append(row_d * fx_wy + row_w * fy_dy)
            l2.append(row_w * fz_wy)
        l1_hi, l1_lo = split3(jnp.concatenate(l1, axis=0))
        l2_hi, l2_lo = split3(jnp.concatenate(l2, axis=0))
        both = dot(jnp.concatenate([l1_hi, l2_hi], axis=1), right)
        rest = dot(jnp.concatenate([l1_lo, l2_lo], axis=1), right_hi)
        r = (both[:, 0:128] + both[:, 128:256] + rest).reshape(7, 48, 128)
        for k in range(7):
            i = t * 7 + k
            share = r[k] * (dom[...] * x_in(ix * W - 5, i, W * NGX))
            if 5 <= i < W + 5:
                g_out[i + 4, 0:W, :] = share[0:W] + rv[i - 5]
                g_out[i + 4, W:48, :] = share[W:48]
            else:
                g_out[i + 4] = share

    zero = jnp.zeros((48, 128), F32)
    for i in (0, 1, 2, 3, 46, 47, 48, 49):
        g_out[i] = zero
    vt[0] = zero
    vt[49] = zero
    double_sweep(vt, g_out, 1, 49, 1, dom, ix * W - 9, W * NGX)

    def emit(k, u, r):
        tmp1[k] = r

    restrict_rows(emit, vt, g_out, tmp, 0, 24, 1, 1, 24)
    even = (lanes((24, 128)) & 1) == 0
    for k in range(12):
        own = jnp.where(even, tmp1[2 * k], tmp1[2 * k + 1])
        own_out[k] = own
        to_hi = own[4:20]
        to_lo = jnp.concatenate([own[20:24], own[0:12]], axis=0)
        c_out[k] = jnp.where(py == 0, to_hi, to_lo)
        d_out[k] = jnp.where(py == 0, to_lo, to_hi)
    for out in (c_out, d_out):
        out[12] = f_out[0:16, :]
        out[13] = f_out[16:32, :]


def pack_g(info, g, cg_out, dg_out):
    ix, iy, px, py = place(info)
    for i in range(42):
        to_hi = g[i + 4, 24:40, :]
        to_lo = jnp.concatenate([g[i + 4, 40:48, :], g[i + 4, 0:8, :]], axis=0)
        cg_out[i] = jnp.where(py == 0, to_hi, to_lo)
        dg_out[i] = jnp.where(py == 0, to_lo, to_hi)


def merge_g(info, g, c_in, d_in, h_out, a_out, b_out):
    ix, iy, px, py = place(info)
    ok_hi, ok_lo = okf(iy < NGY - 1), okf(iy > 0)

    def body(i, u):
        hi, lo = hi_lo(py, c_in[i], d_in[i])
        hi, lo = hi * ok_hi, lo * ok_lo
        v = g[i + 4]
        h_out[i, 0:8, :] = v[0:8] + lo[8:16]
        h_out[i, 8:24, :] = v[8:24]
        h_out[i, 24:40, :] = v[24:40] + hi
        h_out[i, 40:48, :] = v[40:48] + lo[0:8]

    rows(0, 42, 42, body)
    off_a = jnp.where(px == 0, 31, 0)
    off_b = 31 - off_a

    def pack(k, u):
        a_out[k] = h_out[off_a + k]
        b_out[k] = h_out[off_b + k]

    rows(0, 11, 11, pack)


def emit_level1(own_out, c_out, d_out, py, tmp1, v2, b, tmp):
    lane = lanes((16, 128))

    def emit(k, u, r):
        tmp1[k] = r

    restrict_rows(emit, v2, b, tmp, 0, 16, 6, 1, 16)
    for k in range(8):
        own = jnp.where((lane & 1) == 0, tmp1[2 * k], tmp1[2 * k + 1])
        own_out[k] = own
        c_out[k] = jnp.where(py == 0, own[8:16], own[0:8])
        d_out[k] = jnp.where(py == 0, own[0:8], own[8:16])


def down0(info, h, a_in, b_in, b_out, dom):
    ix, iy, px, py = place(info)
    okx_hi, okx_lo = okf(ix < NGX - 1), okf(ix > 0)
    dom[...] = y_domain(48, W, 8, iy * W, W * NGY)
    start = ix * W - 6

    def inner(i, u):
        b_out[i] = h[i - 1] * dom[...] * x_in(start, i, W * NGX)

    rows(1, 43, 42, inner)
    zero = jnp.zeros((48, 128), F32)
    b_out[0] = zero
    b_out[43] = zero

    def rim(k, u):
        hi, lo = hi_lo(px, a_in[k], b_in[k])
        b_out[k] = b_out[k] + lo * dom[...] * (okx_lo * x_in(start, k, W * NGX))
        j = k + 33
        b_out[j] = b_out[j] + hi * dom[...] * (okx_hi * x_in(start, j, W * NGX))

    rows(0, 11, 11, rim)


def merge1_gx(info, own, f, c_in, d_in, s_out, a_out, b_out):
    ix, iy, px, py = place(info)
    ok_hi, ok_lo = okf(iy < NGY - 1), okf(iy > 0)
    for k in range(12):
        hi, lo = hi_lo(py, c_in[k], d_in[k])
        hi, lo = hi * ok_hi, lo * ok_lo
        s_out[k, 0:4, :] = own[k, 0:4, :] + lo[12:16]
        s_out[k, 4:12, :] = own[k, 4:12, :]
        s_out[k, 12:20, :] = own[k, 12:20, :] + hi[0:8]
        s_out[k, 20:28, :] = hi[8:16]
        s_out[k, 28:36, :] = jnp.zeros((8, 128), F32)
        s_out[k, 36:44, :] = lo[0:8]
        s_out[k, 44:48, :] = own[k, 20:24, :] + lo[8:12]
    off_a = jnp.where(px == 0, 5, 0)
    off_b = 5 - off_a
    for out, off in ((a_out, off_a), (b_out, off_b)):
        for k in range(7):
            out[k, 0:28, :] = s_out[off + k, 0:28, :]
            out[k, 28:40, :] = s_out[off + k, 36:48, :]
        for n in range(2):
            hi, lo = hi_lo(py, c_in[12 + n], d_in[12 + n])
            out[7 + n, 0:16, :] = f[16 * n : 16 * n + 16, :]
            out[7 + n, 16:32, :] = hi
            out[9, 16 * n : 16 * n + 16, :] = lo
        out[7, 32:40, :] = jnp.zeros((8, 128), F32)
        out[8, 32:40, :] = jnp.zeros((8, 128), F32)
        out[9, 32:40, :] = jnp.zeros((8, 128), F32)


def down1_shares(info, shares, f, c_in, d_in, a_in, b_in, pairs, packed, f9, s_b1, s_v1, s_b2, s_v2, dom1, dom2, tmp, tmp3):
    ix, iy, px, py = place(info)
    okx_hi, okx_lo = okf(ix < NGX - 1), okf(ix > 0)
    dom1[...] = y_domain(48, 16, 16, iy * 16, W * NGY // 2)
    start1, n1x = ix * 16 - 10, W * NGX // 2
    gap = jnp.zeros((8, 128), F32)

    def wide_y(v):
        return jnp.concatenate([v[0:28], gap, v[28:40]], axis=0)

    for p in range(18):
        total = None
        if 3 <= p < 15:
            total = shares[p - 3]
        if p < 7:
            part = wide_y(hi_lo(px, a_in[p], b_in[p])[1] * okx_lo)
            total = part if total is None else total + part
        if p >= 11:
            part = wide_y(hi_lo(px, a_in[p - 11], b_in[p - 11])[0] * okx_hi)
            total = part if total is None else total + part
        pairs[p] = total * (dom1[...] * x_in(start1, 2 * p, n1x))
    levels_down(info, pairs, s_b1, s_v1, s_b2, s_v2, dom1, dom2, tmp)
    pack3(packed, s_b2, s_v2, tmp, tmp3)
    for n in range(2):
        rows16 = slice(16 * n, 16 * n + 16)
        f9[0, rows16, :] = f[rows16, :]
        hi, lo = hi_lo(py, c_in[12 + n], d_in[12 + n])
        f9[1, rows16, :] = hi
        f9[2, rows16, :] = lo
        hi, lo = hi_lo(px, a_in[7 + n], b_in[7 + n])
        for m in range(2):
            f9[3 + m, rows16, :] = hi[16 * m : 16 * m + 16]
            f9[6 + m, rows16, :] = lo[16 * m : 16 * m + 16]
    hi, lo = hi_lo(px, a_in[9], b_in[9])
    f9[5] = hi[0:32]
    f9[8] = lo[0:32]


def pack1_gx(info, own, c_in, d_in, a_out, b_out):
    ix, iy, px, py = place(info)
    ok_hi, ok_lo = okf(iy < NGY - 1), okf(iy > 0)
    off_a = jnp.where(px == 0, 4, 0)
    off_b = 4 - off_a
    for out, off in ((a_out, off_a), (b_out, off_b)):
        for k in range(4):
            hi, lo = hi_lo(py, c_in[off + k], d_in[off + k])
            out[k, 0:16, :] = own[off + k]
            out[k, 16:24, :] = hi * ok_hi
            out[k, 24:32, :] = lo * ok_lo


def down1(info, own, c_in, d_in, a_in, b_in, pairs, packed, s_b1, s_v1, s_b2, s_v2, dom1, dom2, tmp, tmp3):
    ix, iy, px, py = place(info)
    ok_hi, ok_lo = okf(iy < NGY - 1), okf(iy > 0)
    okx_hi, okx_lo = okf(ix < NGX - 1), okf(ix > 0)
    gap = jnp.zeros((16, 128), F32)
    for k in range(18):
        pairs[k, 24:40, :] = gap
    zero = jnp.zeros((48, 128), F32)
    pairs[0] = zero
    pairs[17] = zero
    for k in range(8):
        hi, lo = hi_lo(py, c_in[k], d_in[k])
        pairs[5 + k, 0:16, :] = own[k]
        pairs[5 + k, 16:24, :] = hi * ok_hi
        pairs[5 + k, 40:48, :] = lo * ok_lo
    for k in range(4):
        hi, lo = hi_lo(px, a_in[k], b_in[k])
        pairs[1 + k, 0:24, :] = lo[0:24] * okx_lo
        pairs[1 + k, 40:48, :] = lo[24:32] * okx_lo
        pairs[13 + k, 0:24, :] = hi[0:24] * okx_hi
        pairs[13 + k, 40:48, :] = hi[24:32] * okx_hi
    levels_down(info, pairs, s_b1, s_v1, s_b2, s_v2, dom1, dom2, tmp)
    pack3(packed, s_b2, s_v2, tmp, tmp3)


def levels_down(info, pairs, b1, v1, b2, v2, dom1, dom2, tmp):
    ix, iy, px, py = place(info)
    n1x, n1y = W * NGX // 2, W * NGY // 2
    dom1[...] = y_domain(48, 16, 16, iy * 16, n1y)
    dom2[...] = y_domain(24, 8, 8, iy * 8, n1y // 2)
    even = (lanes((48, 128)) & 1) == 0
    for k in range(18):
        p = pairs[k]
        b1[2 * k] = jnp.where(even, p, pltpu.roll(p, 1, 1))
        b1[2 * k + 1] = jnp.where(even, pltpu.roll(p, 127, 1), p)
    zero1 = jnp.zeros((48, 128), F32)
    v1[0] = zero1
    v1[35] = zero1
    start1 = ix * 16 - 10
    double_sweep(v1, b1, 1, 35, 2, dom1, start1, n1x)
    start2 = ix * 8 - 4

    def emit2(k, u, r):
        b2[k] = r * dom2[...] * x_in(start2, k, n1x // 2)

    restrict_rows(emit2, v1, b1, tmp, 0, 16, 2, 2, 24)
    zero2 = jnp.zeros((24, 128), F32)
    v2[0] = zero2
    v2[15] = zero2
    double_sweep(v2, b2, 1, 15, 4, dom2, start2, n1x // 2)


def pack3(packed, b2, v2, tmp, tmp3):
    def emit3(k, u, r):
        tmp3[k] = r

    restrict_rows(emit3, v2, b2, tmp, 0, 4, 4, 4, 8)
    row = lax.broadcasted_iota(jnp.int32, (8, 128), 0)
    lane = lanes((8, 128)) & 7
    first = okf((lane == row) & (row < 4))
    second = okf((lane == row + 4) & (row < 4))
    for q in range(2):
        s = tmp3[2 * q] * first + tmp3[2 * q + 1] * second
        tmp3[4 + q, 0:1, :] = jnp.sum(s, axis=0, keepdims=True)
    both = jnp.concatenate([tmp3[4, 0:1, :], tmp3[5, 0:1, :]], axis=0)
    packed[...] = jnp.broadcast_to(both[None], packed.shape)


def again(info, pairs, v0, b1, v1, b2, v2, v_out, dom1, dom2, tmp):
    for i in range(44):
        v_out[i] = v0[i]
    levels_down(info, pairs, b1, v1, b2, v2, dom1, dom2, tmp)


def coarse_up(info, g, pairs, s, ready=None):
    ix, iy, px, py = place(info)
    n3x = NGX * 4

    def load(d, u):
        at = ix - 7 + d
        ok = okf((at >= 0) & (at < NGX))
        at = jnp.clip(at, 0, NGX - 1)
        base = d * 16
        s.px[pl.ds(pl.multiple_of(base, 8), 8), :] = g[at, pl.ds(0, 8, stride=2), :] * ok
        s.px[pl.ds(pl.multiple_of(base + 8, 8), 8), :] = g[at, pl.ds(1, 8, stride=2), :] * ok

    rows(0, 15, 15, load)
    src = lax.broadcasted_iota(jnp.int32, (128, 1024), 0)
    dst = lax.broadcasted_iota(jnp.int32, (128, 1024), 1)
    pick = okf(src == ((dst & 127) >> 3) * 8 + (dst >> 7)).astype(BF16)
    x = s.px[...]
    x_hi, x_lo = split3(x)
    x_lo2 = (x - x_hi.astype(F32) - x_lo.astype(F32)).astype(BF16)
    s.pu[...] = dot(x_hi, pick) + dot(x_lo, pick) + dot(x_lo2, pick)

    def place3(d, u):
        for q in range(2):
            for j in range(8):
                part = s.pu[pl.ds(pl.multiple_of(d * 16 + q * 8, 8), 8), j * 128 : (j + 1) * 128]
                s.b3[d * 4 + 2 * q + (j >> 2), pl.ds(j & 3, 8, stride=4), :] = part

    rows(0, 15, 15, place3)
    e3, e4, e5 = y_edge(32), y_edge(16), y_edge(8)
    start3, start4, start5 = (ix - 7) * 4, (ix - 7) * 2, ix - 7
    z3, z4, z5 = jnp.zeros((32, 128), F32), jnp.zeros((16, 128), F32), jnp.zeros((8, 128), F32)
    for r, z, n in ((s.v3, z3, 60), (s.b4, z4, 30), (s.v4, z4, 30), (s.b5, z5, 15), (s.v5, z5, 15), (s.w5, z5, 15)):
        r[0] = z
        r[n - 1] = z
    double_sweep(s.v3, s.b3, 1, 59, 8, None, start3, n3x, e3)

    def emit4(k, u, r):
        s.b4[k] = r * x_in(start4, k, n3x // 2)

    restrict_rows(emit4, s.v3, s.b3, s.tmp, 1, 29, 0, 8, 16, e3)
    double_sweep(s.v4, s.b4, 1, 29, 16, None, start4, n3x // 2, e4)

    def emit5(k, u, r):
        s.b5[k] = r * x_in(start5, k, NGX)

    restrict_rows(emit5, s.v4, s.b4, s.tmp, 1, 14, 0, 16, 8, e4)
    double_sweep(s.v5, s.b5, 1, 14, 32, None, start5, NGX, e5)
    sweep(s.w5, s.v5, s.b5, 1, 14, 32, None, start5, NGX, e5)
    sweep(s.v5, s.w5, s.b5, 1, 14, 32, None, start5, NGX, e5)

    correct(s.w4, s.v4, s.v5, s.tmp, 5, 10, 0, ((0, 8, 0),), 16, None, start4, n3x // 2)
    sweep(s.v4, s.w4, s.b4, 11, 19, 16, None, start4, n3x // 2, e4)
    correct(s.w3, s.v3, s.v4, s.tmp, 12, 18, 0, ((0, 16, 0),), 32, None, start3, n3x)
    sweep(s.v3, s.w3, s.b3, 26, 34, 8, None, start3, n3x, e3)

    if ready is None:
        levels_down(info, use(pairs), s.b1, s.v1, s.b2, s.v2, s.dom1, s.dom2, s.tmp)
    else:
        s.b1, s.v1, s.b2, s.v2 = [use(r) for r in ready]
        s.dom1[...] = y_domain(48, 16, 16, iy * 16, NGY * 16)
        s.dom2[...] = y_domain(24, 8, 8, iy * 8, NGY * 8)
    turn = lax.rem(32 - 4 * iy, 32)

    def shifted(k):
        return pltpu.roll(s.v3[k + 26], turn, 0)

    start2, start1 = ix * 8 - 4, ix * 16 - 10
    n2x, n1x = n3x * 2, n3x * 4
    correct(s.w2, s.v2, None, s.tmp, 0, 8, 0, ((0, 8, 0), (28, 4, 16)), 24, s.dom2, start2, n2x, shifted)
    sweep(s.e2, s.w2, s.b2, 2, 14, 4, s.dom2, start2, n2x)
    correct(s.w1, s.v1, s.e2, s.tmp, 2, 14, 2, ((0, 24, 0),), 48, s.dom1, start1, n1x)
    sweep(s.e1, s.w1, s.b1, 7, 29, 2, s.dom1, start1, n1x)


class Bag:
    pass


COARSE = (
    ("px", (240, 128)),
    ("pu", (240, 1024)),
    ("b3", (60, 32, 128)),
    ("v3", (60, 32, 128)),
    ("w3", (60, 32, 128)),
    ("b4", (30, 16, 128)),
    ("v4", (30, 16, 128)),
    ("w4", (30, 16, 128)),
    ("b5", (15, 8, 128)),
    ("v5", (15, 8, 128)),
    ("w5", (15, 8, 128)),
    ("w2", (16, 24, 128)),
    ("e2", (16, 24, 128)),
    ("w1", (36, 48, 128)),
    ("e1", (36, 48, 128)),
    ("w0", (44, 48, 128)),
    ("x0", (44, 48, 128)),
    ("dom0", (48, 128)),
    ("dom1", (48, 128)),
    ("dom2", (24, 128)),
    ("b1", (36, 48, 128)),
    ("v1", (36, 48, 128)),
    ("b2", (16, 24, 128)),
    ("v2", (16, 24, 128)),
    ("v0", (44, 48, 128)),
    ("tmp", (32, 48, 128)),
    ("tmp1", (16, 16, 128)),
)
COARSE_SCRATCH = [pltpu.VMEM(shape, F32) for name, shape in COARSE]


OUT_SCRATCH = [pltpu.VMEM((3, W, W, 128), F32), pltpu.VMEM((W, W, 128), F32), pltpu.SemaphoreType.DMA((8,))]


def bag(refs):
    s = Bag()
    for (name, shape), ref in zip(COARSE, refs):
        setattr(s, name, ref)
    return s


PIECES0 = ((0, 20, 0), (44, 4, 40))


def middle(info, g, b0, pairs, v_out, own_out, c_out, d_out, *scratch):
    s = bag(scratch)
    ix, iy, px, py = place(info)
    coarse_up(info, g, pairs, s)
    s.dom0[...] = y_domain(48, W, 8, iy * W, W * NGY)
    start, size = ix * W - 6, W * NGX
    b0 = use(b0)
    zero = jnp.zeros((48, 128), F32)
    s.v0[0] = zero
    s.v0[43] = zero
    double_sweep(s.v0, b0, 1, 43, 1, s.dom0, start, size)
    correct(s.w0, s.v0, s.e1, s.tmp, 7, 29, -14, PIECES0, 48, s.dom0, start, size)
    sweep(s.x0, s.w0, b0, 2, 42, 1, s.dom0, start, size)
    sweep(s.w0, s.x0, b0, 3, 41, 1, s.dom0, start, size)
    sweep(v_out, s.w0, b0, 4, 40, 1, s.dom0, start, size)
    for i in (0, 1, 2, 3, 40, 41, 42, 43):
        v_out[i] = zero
    emit_level1(own_out, c_out, d_out, py, s.tmp1, v_out, b0, s.tmp)


def final(info, g, b0, v0, b1, v1, b2, v2, pushed, vel_out, p_out, vel_buf, p_buf, sems, *scratch):
    s = bag(scratch)
    ix, iy, px, py = place(info)
    coarse_up(info, g, None, s, (b1, v1, b2, v2))
    s.dom0[...] = y_domain(48, W, 8, iy * W, W * NGY)
    start, size = ix * W - 6, W * NGX
    b0, v0 = use(b0), use(v0)
    correct(s.w0, v0, s.e1, s.tmp, 9, 27, -14, PIECES0, 48, s.dom0, start, size)
    sweep(s.x0, s.w0, b0, 5, 39, 1, s.dom0, start, size)
    zm = z_masks(1)
    pushed = use(pushed)
    copies = []
    for t in range(4):
        for x in range(8 * t, 8 * t + 8):
            p = s.x0[x + 6]
            own = p[0:W]
            p_buf[x] = own
            gx = s.x0[x + 7, 0:W, :] - s.x0[x + 5, 0:W, :]
            gy = pltpu.roll(p, 47, 0)[0:W] - pltpu.roll(p, 1, 0)[0:W]
            gz = pltpu.roll(own, 127, 1) * zm[1] - pltpu.roll(own, 1, 1) * zm[0]
            vel_buf[0, x] = pushed[0, x] - 0.5 * gx
            vel_buf[1, x] = pushed[1, x] - 0.5 * gy
            vel_buf[2, x] = pushed[2, x] - 0.5 * gz
        part = pl.ds(8 * t, 8)
        copies.append(pltpu.make_async_copy(vel_buf.at[:, part], vel_out.at[:, part], sems.at[2 * t]))
        copies.append(pltpu.make_async_copy(p_buf.at[part], p_out.at[part], sems.at[2 * t + 1]))
        copies[-2].start()
        copies[-1].start()
    for copy in copies:
        copy.wait()


def push_kernel(info, vel, f9, out):
    ix, iy, px, py = place(info)
    ok = {-1: (okf(ix > 0), okf(iy > 0)), 0: (1.0, 1.0), 1: (okf(ix < NGX - 1), okf(iy < NGY - 1))}
    start_x = (ix * W).astype(F32)
    start_y = (iy * W).astype(F32)
    order = ((0, 0), (0, 1), (0, -1), (1, 0), (1, 1), (1, -1), (-1, 0), (-1, 1), (-1, -1))
    for slot, (ox_, oy_) in enumerate(order):
        q = f9.at[slot]
        cx, cy, cz = vec(q, 6) - start_x, vec(q, 8) - start_y, vec(q, 10)
        ox, oy, oz = vec(q, 12), vec(q, 14), vec(q, 16)
        keep = ok[ox_][0] * ok[oy_][1]
        force = [vec(q, 2 * c) * keep for c in range(3)]
        wx = taps(row_coord(32, 0), cx, ox, tap_norm(ox))
        y0, yn = {0: (0, 32), 1: (24, 8), -1: (0, 8)}[oy_]
        wy = taps(row_coord(yn, y0), cy, oy, tap_norm(oy))
        wz = taps(row_coord(128, 0), cz, oz, tap_norm(oz)).T
        r_hi, r_lo = split3(wz)
        right = jnp.concatenate([r_hi, r_lo, r_hi], axis=0)
        fy = [force[c] * wy for c in range(3)]
        x0, xn = {0: (0, 32), 1: (28, 4), -1: (0, 4)}[ox_]
        step = min(xn, 4 if oy_ == 0 else 16)

        def spread(t, x0=x0, step=step, fy=fy, right=right, y0=y0, yn=yn, slot=slot, wx=wx):
            at = x0 + t * step
            left = []
            for k in range(step):
                row = wx[at + k : at + k + 1, :]
                left += [row * fy[c] for c in range(3)]
            hi, lo = split3(jnp.concatenate(left, axis=0))
            r = dot(jnp.concatenate([hi, hi, lo], axis=1), right).reshape(step, 3, yn, 128)
            for k in range(step):
                for c in range(3):
                    base = vel if slot == 0 else out
                    out[c, at + k, y0 : y0 + yn, :] = base[c, at + k, y0 : y0 + yn, :] + r[k, c]

        for t in range(xn // step):
            spread(t)


def gather3(packed):
    return lax.all_to_all(packed, AXES, 0, 0, tiled=True).reshape(NGX, 16, 128)


LEVELS12 = [(18, 48, 128), (NGX * NGY, 2, 128)]
DOWN1 = [
    VMEM((36, 48, 128), F32), VMEM((36, 48, 128), F32), VMEM((16, 24, 128), F32), VMEM((16, 24, 128), F32),
    VMEM((48, 128), F32), VMEM((24, 128), F32), VMEM((32, 48, 128), F32), VMEM((6, 8, 128), F32),
]


def per_device(velocity, point_cells, point_offsets, point_count, drag, blade_speed):
    info = jnp.stack([lax.axis_index("gx"), lax.axis_index("gy"), point_count.reshape(())]).astype(jnp.int32)

    py = lax.axis_index("gy") % 2
    top, bottom = velocity[:, :, W - 4 :, :].reshape(3 * W, 4, 128), velocity[:, :, :4, :].reshape(3 * W, 4, 128)
    c0, d0 = swap_gy(jnp.where(py == 0, top, bottom), jnp.where(py == 0, bottom, top))
    a0, b0 = call(pack_gx, [(12, 40, 128)] * 2, [], info, velocity[:, :4], velocity[:, W - 4 :], c0, d0)
    a0, b0 = swap_gx(a0, b0)
    part, xt, yt, zt = call(
        sample_kernel, [(3, 40, P_), (2, 48, P_), (2, 48, P_), (2, P_, 128)], [], info, velocity, point_cells, point_offsets, c0, d0
    )
    g, f, own1, c1, d1 = call(
        force_kernel,
        [(50, 48, 128), (32, 128), (12, 24, 128), (14, 16, 128), (14, 16, 128)],
        [
            VMEM((3, 40, 40, 128), F32), VMEM((W, W, 128), F32), VMEM((50, 48, 128), F32), VMEM((48, 128), F32),
            VMEM((32, 48, 128), F32), VMEM((24, 24, 128), F32),
        ],
        info, velocity, point_cells, point_offsets, drag, blade_speed, part, xt, yt, zt, c0, d0, a0, b0,
    )
    c1, d1 = swap_gy(c1, d1)
    shares, a1, b1 = call(merge1_gx, [(12, 48, 128), (10, 40, 128), (10, 40, 128)], [], info, own1, f, c1, d1)
    a1, b1 = swap_gx(a1, b1)
    pairs, packed, f9 = call(down1_shares, LEVELS12 + [(9, 32, 128)], DOWN1, info, shares, f, c1, d1, a1, b1)
    cg, dg = call(pack_g, [(42, 16, 128)] * 2, [], info, g)
    packed, g, cg, dg, f9 = lax.optimization_barrier((packed, g, cg, dg, f9))
    gathered = gather3(packed)
    cg, dg = swap_gy(cg, dg)
    h, ag, bg = call(merge_g, [(42, 48, 128), (11, 48, 128), (11, 48, 128)], [], info, g, cg, dg)
    ag, bg = swap_gx(ag, bg)
    (rhs,) = call(down0, [(44, 48, 128)], [VMEM((48, 128), F32)], info, h, ag, bg)
    v0, own1, c1, d1 = call(
        middle, [(44, 48, 128), (8, 16, 128), (8, 8, 128), (8, 8, 128)], COARSE_SCRATCH, info, gathered, rhs, pairs
    )
    c1, d1 = swap_gy(c1, d1)
    a1, b1 = call(pack1_gx, [(4, 32, 128)] * 2, [], info, own1, c1, d1)
    a1, b1 = swap_gx(a1, b1)
    pairs, packed = call(down1, LEVELS12, DOWN1, info, own1, c1, d1, a1, b1)
    packed, pairs, v0 = lax.optimization_barrier((packed, pairs, v0))
    gathered = gather3(packed)
    *levels, v0 = call(
        again, [(36, 48, 128), (36, 48, 128), (16, 24, 128), (16, 24, 128), (44, 48, 128)],
        [VMEM((48, 128), F32), VMEM((24, 128), F32), VMEM((32, 48, 128), F32)], info, pairs, v0,
    )
    (pushed,) = call(push_kernel, [(3, W, W, 128)], [], info, velocity, f9)
    vel_out, p_out = call(
        final, [(3, W, W, 128), (W, W, 128)], OUT_SCRATCH + COARSE_SCRATCH, info, gathered, rhs, v0, *levels, pushed,
        late=(2, 3, 4, 5, 6, 7, 8), direct=(0, 1),
    )
    return vel_out, p_out


def solution(mesh):
    placed = (
        P(None, "gx", "gy", None),
        P(None, "gx", "gy", None),
        P(None, "gx", "gy", None),
        P("gx", "gy"),
        P("gx", "gy", None),
        P("gx", "gy", None),
    )
    return jax.shard_map(
        per_device,
        mesh=mesh,
        in_specs=placed,
        out_specs=(P(None, "gx", "gy", None), P("gx", "gy", None)),
        check_vma=False,
    )
```

```python
import functools

import jax
import jax.numpy as jnp
from jax import lax
from jax.experimental import pallas as pl
from jax.experimental.pallas import tpu as pltpu
from jax.sharding import PartitionSpec as P

AXES = ("gx", "gy")
NGX, NGY = 32, 8
W = 32
P_ = 256
F32 = jnp.float32
BF16 = jnp.bfloat16
VMEM = pltpu.VMEM
LIMIT = 24 * 1024 * 1024
WHOLE = 60 * 1024 * 1024


def swap(x, fx, fy):
    perm = [(i * NGY + j, fx(i) * NGY + fy(j)) for i in range(NGX) for j in range(NGY)]
    return lax.ppermute(x, AXES, perm)


def same(i):
    return i


def pair(i):
    return i ^ 1


def other(n):
    return lambda i: (i + 1) % n if i % 2 else (i - 1) % n


def swap_gx(a, b):
    return swap(a, pair, same), swap(b, other(NGX), same)


def swap_gy(c, d):
    return swap(c, same, pair), swap(d, same, other(NGY))


class Late:
    def __init__(self, copy, ref):
        self.copy, self.ref, self.done = copy, ref, False

    def get(self):
        if not self.done:
            self.copy.wait()
            self.done = True
        return self.ref


def use(x):
    return x.get() if isinstance(x, Late) else x


class Early:
    def __init__(self, copy, ref):
        self.copy, self.ref, self.sent = copy, ref, False

    def flush(self):
        if not self.sent:
            self.copy.start()
            self.sent = True


def call(kernel, out_shapes, scratch, *args, late=(), early=(), direct=()):
    nbytes = sum(a.size * 4 for a in args) + sum(4 * functools.reduce(lambda x, y: x * y, s) for s in out_shapes)
    n_in, n_out = len(args), len(out_shapes)

    def body(*refs):
        ins, outs = list(refs[:n_in]), list(refs[n_in : n_in + n_out])
        rest = refs[n_in + n_out :]
        own, rest = rest[: len(scratch)], rest[len(scratch) :]
        if late or early:
            bufs, sems = rest[:-1], rest[-1]
        for n, at in enumerate(late):
            copy = pltpu.make_async_copy(ins[at], bufs[n], sems.at[n])
            copy.start()
            ins[at] = Late(copy, bufs[n])
        for n, at in enumerate(early):
            k = len(late) + n
            outs[at] = Early(pltpu.make_async_copy(bufs[k], outs[at], sems.at[k]), bufs[k])
        kernel(*ins, *outs, *own)
        for at in late:
            use(ins[at])
        for at in early:
            outs[at].flush()
        for at in early:
            outs[at].copy.wait()

    specs = [pl.BlockSpec(memory_space=pltpu.SMEM)] + [
        pl.BlockSpec(memory_space=pltpu.HBM if n in late else VMEM) for n in range(1, n_in)
    ]
    extra = [VMEM(args[n].shape, args[n].dtype) for n in late] + [VMEM(out_shapes[n], F32) for n in early]
    if extra:
        extra.append(pltpu.SemaphoreType.DMA((len(extra),)))
    return pl.pallas_call(
        body,
        out_shape=[jax.ShapeDtypeStruct(s, F32) for s in out_shapes],
        in_specs=specs,
        out_specs=[pl.BlockSpec(memory_space=pltpu.HBM if n in early or n in direct else VMEM) for n in range(n_out)],
        scratch_shapes=list(scratch) + extra,
        compiler_params=pltpu.CompilerParams(vmem_limit_bytes=WHOLE if late else LIMIT),
        cost_estimate=pl.CostEstimate(flops=10_000_000, bytes_accessed=nbytes, transcendentals=0),
    )(*args)


def rows(lo, hi, unroll, body):
    n = hi - lo
    main = n // unroll if unroll < n else 0
    if main > 1:

        def step(t, c):
            for u in range(unroll):
                body(lo + t * unroll + u, u)
            return c

        lax.fori_loop(0, main, step, 0)
        lo = lo + main * unroll
    for i in range(lo, hi):
        body(i, i - lo)


def place(info):
    ix, iy = info[0], info[1]
    return ix, iy, ix % 2, iy % 2


def okf(cond):
    return jnp.where(cond, 1.0, 0.0).astype(F32)


def hi_lo(par, a, b):
    return jnp.where(par == 0, a, b), jnp.where(par == 0, b, a)


def lanes(shape=(1, 128)):
    return lax.broadcasted_iota(jnp.int32, shape, len(shape) - 1)


def z_masks(s):
    lane = lanes()
    return okf(lane >= s), okf(lane < 128 - s)


def neighbours(ref, i, v, s, zm, ym=None):
    size = v.shape[0]
    up = pltpu.roll(v, 1, 0)
    down = pltpu.roll(v, size - 1, 0)
    if ym is not None:
        up, down = up * ym[0], down * ym[1]
    low = pltpu.roll(v, s, 1) * zm[0]
    high = pltpu.roll(v, 128 - s, 1) * zm[1]
    return (ref[i - 1] + ref[i + 1]) + (up + down) + (low + high)


def x_in(start, i, size):
    g = start + i
    return okf((g >= 0) & (g < size))


def y_edge(size):
    r = lax.broadcasted_iota(jnp.int32, (size, 1), 0)
    return okf(r > 0), okf(r < size - 1)


def y_domain(size, own, hi, start, total):
    r = lax.broadcasted_iota(jnp.int32, (size, 128), 0)
    g = start + jnp.where(r < own + hi, r, r - size)
    return okf((g >= 0) & (g < total))


def double_sweep(dst, b, lo, hi, s, dom, start, size, ym=None, unroll=64):
    zm = z_masks(s)

    def body(i, u):
        v = b[i]
        c = x_in(start, i, size) * (1.0 / 49.0)
        out = (8.0 * v + neighbours(b, i, v, s, zm, ym)) * c
        if dom is not None:
            out = out * dom[...]
        dst[i] = out

    rows(lo, hi, unroll, body)


def sweep(dst, v_ref, b, lo, hi, s, dom, start, size, ym=None, unroll=64):
    zm = z_masks(s)

    def body(i, u):
        v = v_ref[i]
        c = x_in(start, i, size) * (1.0 / 7.0)
        out = (v + b[i] + neighbours(v_ref, i, v, s, zm, ym)) * c
        if dom is not None:
            out = out * dom[...]
        dst[i] = out

    rows(lo, hi, unroll, body)


def z_pairs(t, s):
    lane = lanes(t.shape)
    return t + jnp.where((lane & s) == 0, pltpu.roll(t, 128 - s, 1), pltpu.roll(t, s, 1))


def restrict_rows(emit, v_ref, b, tmp, klo, khi, base, s, keep, ym=None, unroll=64):
    zm = z_masks(s)

    def first(k, u):
        i = base + 2 * k
        total = None
        for d in range(2):
            v = v_ref[i + d]
            r = b[i + d] - 6.0 * v + neighbours(v_ref, i + d, v, s, zm, ym)
            total = r if total is None else total + r
        tmp[u, 0 : total.shape[0], :] = total

    def second(k, u):
        both = tmp[u, pl.ds(0, keep, stride=2), :] + tmp[u, pl.ds(1, keep, stride=2), :]
        emit(k, u, z_pairs(both, s) * 0.5)

    rows(klo, khi, unroll, first)
    rows(klo, khi, unroll, second)


def correct(dst, v_ref, e_ref, tmp, klo, khi, base, pieces, size, dom, start, total, get=None, unroll=64):
    def first(k, u):
        e = e_ref[k] if get is None else get(k)
        for at, count, to in pieces:
            part = e[at : at + count]
            tmp[u, pl.ds(to, count, stride=2), :] = part
            tmp[u, pl.ds(to + 1, count, stride=2), :] = part

    def second(k, u):
        wide = tmp[u, 0:size, :]
        for d in range(2):
            i = base + 2 * k + d
            out = v_ref[i] + wide
            if dom is not None:
                out = out * dom[...]
            dst[i] = out * x_in(start, i, total)

    rows(klo, khi, unroll, first)
    rows(klo, khi, unroll, second)


def split3(x):
    hi = x.astype(BF16)
    lo = (x - hi.astype(F32)).astype(BF16)
    return hi, lo


def dot(a, b):
    return jnp.dot(a, b, preferred_element_type=F32)


def vec(ref, at):
    return jnp.concatenate([ref[at : at + 1, :], ref[at + 1 : at + 2, :]], axis=1)


def tap_norm(off):
    total = jnp.zeros_like(off)
    for k in range(-3, 5):
        u = (k - off) / 1.5
        total = total + jnp.exp(-u * u)
    return 1.0 / total


def taps(coord, cell, off, inv, ok=None):
    d = coord - cell
    u = (d - off) / 1.5
    hit = (d >= -3.0) & (d <= 4.0)
    if ok is not None:
        hit = hit & ok
    return jnp.where(hit, jnp.exp(-u * u) * inv, 0.0)


def row_coord(n, shift):
    return (lax.broadcasted_iota(jnp.int32, (n, 1), 0) + shift).astype(F32)


def cyc_coord(n, split):
    r = lax.broadcasted_iota(jnp.int32, (n, 1), 0)
    return jnp.where(r < split, r, r - n).astype(F32)


def pack_gx(info, low, high, c_in, d_in, a_out, b_out):
    ix, iy, px, py = place(info)
    ok_hi, ok_lo = okf(iy < NGY - 1), okf(iy > 0)
    off_a = jnp.where(px == 0, W - 4, 0)
    off_b = W - 4 - off_a
    for out, off in ((a_out, off_a), (b_out, off_b)):
        for c in range(3):
            for k in range(4):
                x = off + k
                e = c * 4 + k
                hi, lo = hi_lo(py, c_in[c * W + x], d_in[c * W + x])
                out[e, 0:W, :] = jnp.where(off > 0, high[c, k], low[c, k])
                out[e, W : W + 4, :] = hi * ok_hi
                out[e, W + 4 : W + 8, :] = lo * ok_lo


def points(info, cells, offs):
    where = [cells[n, 0].astype(F32) for n in range(3)]
    local = [where[0] - (info[0] * W).astype(F32), where[1] - (info[1] * W).astype(F32), where[2]]
    off = [offs[n, 0] for n in range(3)]
    return where, local, off, [tap_norm(o) for o in off]


def sampled_lines(slabs, wx, first, wz3, acc):
    for c in range(3):
        n = slabs[c].shape[0]
        hi, lo = split3(slabs[c].reshape(40 * n, 128))
        r = dot(jnp.concatenate([hi, hi, lo], axis=1), wz3).reshape(n, 40, P_)
        for k in range(n):
            m = r[k] * wx[first + k : first + k + 1, :]
            acc[c] = m if acc[c] is None else acc[c] + m


def z_table(local, off, inv):
    hi, lo = split3(taps(row_coord(128, 0), local[2], off[2], inv[2]))
    return jnp.concatenate([hi, lo, hi], axis=0)


def sample_kernel(info, vel, cells, offs, c_in, d_in, part, xt, yt, zt, rv):
    ix, iy, px, py = place(info)
    ok_hi, ok_lo = okf(iy < NGY - 1), okf(iy > 0)
    where, local, off, inv = points(info, cells, offs)
    wz3 = z_table(local, off, inv)
    wx = taps(row_coord(W, 0), local[0], off[0], inv[0])
    zm = z_masks(1)
    acc = [None] * 3
    for t in range(4):
        slabs = []
        for c in range(3):
            lines = []
            for x in range(t * 8, t * 8 + 8):
                hi, lo = hi_lo(py, c_in[c * W + x], d_in[c * W + x])
                lines.append(jnp.concatenate([vel[c, x], hi * ok_hi, lo * ok_lo], axis=0))
            slabs.append(jnp.stack(lines))
        sampled_lines(slabs, wx, t * 8, wz3, acc)
        for k in range(8):
            x = t * 8 + k
            vy = slabs[1][k]
            total = pltpu.roll(vy, 39, 0)[0:W] - pltpu.roll(vy, 1, 0)[0:W]
            vz = vel[2, x]
            total = total + pltpu.roll(vz, 127, 1) * zm[1] - pltpu.roll(vz, 1, 1) * zm[0]
            if x < W - 1:
                total = total + vel[0, x + 1]
            if x > 0:
                total = total - vel[0, x - 1]
            rv[x] = -0.5 * total
    for c in range(3):
        part[c] = acc[c]

    def axis_taps(d, coord, start, size):
        def at(shift):
            q = coord + shift
            ok = (q + start >= 0.0) & (q + start < size)
            return taps(q, local[d], off[d], inv[d], ok)

        return at(0.0), at(1.0) - at(-1.0)

    xt[0], xt[1] = axis_taps(0, row_coord(48, -5), (ix * W).astype(F32), float(W * NGX))
    yt[0], yt[1] = axis_taps(1, cyc_coord(48, 40), (iy * W).astype(F32), float(W * NGY))
    wz, dz = axis_taps(2, row_coord(128, 0), 0.0, 128.0)
    zt[0] = -0.5 * wz.T
    zt[1] = -0.5 * dz.T


def force_kernel(
    info, cells, offs, drags, blades, part, xt, yt, zt, rv, a_in, b_in,
    g_out, f_out, own_out, c_out, d_out,
    vt, dom, tmp, tmp1,
):
    ix, iy, px, py = place(info)
    ok_hi, ok_lo = okf(iy < NGY - 1), okf(iy > 0)
    okx_hi, okx_lo = okf(ix < NGX - 1), okf(ix > 0)

    slabs = []
    for c in range(3):
        pairs = [hi_lo(px, a_in[c * 4 + k], b_in[c * 4 + k]) for k in range(4)]
        slabs.append(jnp.stack([p[1] * okx_lo for p in pairs] + [p[0] * okx_hi for p in pairs]))
    place_of, local, off, inv = points(info, cells, offs)
    (cx, cy, cz), (ox, oy, oz), (nx, ny, nz) = local, off, inv
    z = row_coord(128, 0)

    wz3 = z_table(local, off, inv)
    rim = row_coord(8, 0)
    wx8 = taps(jnp.where(rim < 4.0, rim - 4.0, rim + (W - 4.0)), cx, ox, nx)
    wy40 = taps(cyc_coord(40, 36), cy, oy, ny)
    acc = [part[c] for c in range(3)]
    sampled_lines(slabs, wx8, 0, wz3, acc)
    sampled = [jnp.sum(acc[c] * wy40, axis=0, keepdims=True) for c in range(3)]
    drag, blade = drags[0], blades[0]
    slot = lax.broadcasted_iota(jnp.int32, (1, P_), 1)
    live = okf(slot < info[2])
    speed = jnp.sqrt(sampled[0] * sampled[0] + sampled[1] * sampled[1] + sampled[2] * sampled[2] + blade * blade)
    pull = -(drag * speed * live)
    force = [pull * s for s in sampled]
    for n, q in enumerate(force + place_of + [ox, oy, oz]):
        f_out[2 * n : 2 * n + 1, :] = q[:, 0:128]
        f_out[2 * n + 1 : 2 * n + 2, :] = q[:, 128:256]
    f_out[18:32, :] = jnp.zeros((14, 128), F32)

    wx, dx, wy, dy = xt[0], xt[1], yt[0], yt[1]
    r1_hi, r1_lo = split3(zt[0])
    r2_hi, r2_lo = split3(zt[1])
    right_hi = jnp.concatenate([r1_hi, r2_hi], axis=0)
    right = jnp.concatenate([right_hi, jnp.concatenate([r1_lo, r2_lo], axis=0)], axis=1)
    fy_dy = force[1] * dy
    fx_wy = force[0] * wy
    fz_wy = force[2] * wy

    dom[...] = y_domain(48, W, 8, iy * W, W * NGY)
    dom[...] = y_domain(48, W, 8, iy * W, W * NGY)
    edge = {0: 0.5 * slabs[0][3, 0:W], W - 1: -0.5 * slabs[0][4, 0:W]}
    for t in range(6):
        l1, l2 = [], []
        for k in range(7):
            i = t * 7 + k
            row_w = wx[i : i + 1, :]
            row_d = dx[i : i + 1, :]
            l1.append(row_d * fx_wy + row_w * fy_dy)
            l2.append(row_w * fz_wy)
        l1_hi, l1_lo = split3(jnp.concatenate(l1, axis=0))
        l2_hi, l2_lo = split3(jnp.concatenate(l2, axis=0))
        both = dot(jnp.concatenate([l1_hi, l2_hi], axis=1), right)
        rest = dot(jnp.concatenate([l1_lo, l2_lo], axis=1), right_hi)
        r = (both[:, 0:128] + both[:, 128:256] + rest).reshape(7, 48, 128)
        for k in range(7):
            i = t * 7 + k
            share = r[k] * (dom[...] * x_in(ix * W - 5, i, W * NGX))
            if 5 <= i < W + 5:
                own = share[0:W] + rv[i - 5]
                g_out[i + 4, 0:W, :] = own + edge[i - 5] if i - 5 in edge else own
                g_out[i + 4, W:48, :] = share[W:48]
            else:
                g_out[i + 4] = share

    zero = jnp.zeros((48, 128), F32)
    for i in (0, 1, 2, 3, 46, 47, 48, 49):
        g_out[i] = zero
    vt[0] = zero
    vt[49] = zero
    double_sweep(vt, g_out, 1, 49, 1, dom, ix * W - 9, W * NGX)

    def emit(k, u, r):
        tmp1[k] = r

    restrict_rows(emit, vt, g_out, tmp, 0, 24, 1, 1, 24)
    even = (lanes((24, 128)) & 1) == 0
    for k in range(12):
        own = jnp.where(even, tmp1[2 * k], tmp1[2 * k + 1])
        own_out[k] = own
        to_hi = own[4:20]
        to_lo = jnp.concatenate([own[20:24], own[0:12]], axis=0)
        c_out[k] = jnp.where(py == 0, to_hi, to_lo)
        d_out[k] = jnp.where(py == 0, to_lo, to_hi)
    for out in (c_out, d_out):
        out[12] = f_out[0:16, :]
        out[13] = f_out[16:32, :]


def pack_g(info, g, cg_out, dg_out):
    ix, iy, px, py = place(info)
    for i in range(42):
        to_hi = g[i + 4, 24:40, :]
        to_lo = jnp.concatenate([g[i + 4, 40:48, :], g[i + 4, 0:8, :]], axis=0)
        cg_out[i] = jnp.where(py == 0, to_hi, to_lo)
        dg_out[i] = jnp.where(py == 0, to_lo, to_hi)


def merge_g(info, g, c_in, d_in, h_out, a_out, b_out):
    ix, iy, px, py = place(info)
    ok_hi, ok_lo = okf(iy < NGY - 1), okf(iy > 0)

    def body(i, u):
        hi, lo = hi_lo(py, c_in[i], d_in[i])
        hi, lo = hi * ok_hi, lo * ok_lo
        v = g[i + 4]
        h_out[i, 0:8, :] = v[0:8] + lo[8:16]
        h_out[i, 8:24, :] = v[8:24]
        h_out[i, 24:40, :] = v[24:40] + hi
        h_out[i, 40:48, :] = v[40:48] + lo[0:8]

    rows(0, 42, 42, body)
    off_a = jnp.where(px == 0, 31, 0)
    off_b = 31 - off_a

    def pack(k, u):
        a_out[k] = h_out[off_a + k]
        b_out[k] = h_out[off_b + k]

    rows(0, 11, 11, pack)


def emit_level1(own_out, c_out, d_out, py, tmp1, v2, b, tmp):
    lane = lanes((16, 128))

    def emit(k, u, r):
        tmp1[k] = r

    restrict_rows(emit, v2, b, tmp, 0, 16, 6, 1, 16)
    for k in range(8):
        own = jnp.where((lane & 1) == 0, tmp1[2 * k], tmp1[2 * k + 1])
        own_out[k] = own
        c_out[k] = jnp.where(py == 0, own[8:16], own[0:8])
        d_out[k] = jnp.where(py == 0, own[0:8], own[8:16])


def down0(info, h, a_in, b_in, b_out, dom):
    ix, iy, px, py = place(info)
    okx_hi, okx_lo = okf(ix < NGX - 1), okf(ix > 0)
    dom[...] = y_domain(48, W, 8, iy * W, W * NGY)
    start = ix * W - 6

    def inner(i, u):
        b_out[i] = h[i - 1] * dom[...] * x_in(start, i, W * NGX)

    rows(1, 43, 42, inner)
    zero = jnp.zeros((48, 128), F32)
    b_out[0] = zero
    b_out[43] = zero

    def rim(k, u):
        hi, lo = hi_lo(px, a_in[k], b_in[k])
        b_out[k] = b_out[k] + lo * dom[...] * (okx_lo * x_in(start, k, W * NGX))
        j = k + 33
        b_out[j] = b_out[j] + hi * dom[...] * (okx_hi * x_in(start, j, W * NGX))

    rows(0, 11, 11, rim)


def merge1_gx(info, own, f, c_in, d_in, s_out, a_out, b_out):
    ix, iy, px, py = place(info)
    ok_hi, ok_lo = okf(iy < NGY - 1), okf(iy > 0)
    for k in range(12):
        hi, lo = hi_lo(py, c_in[k], d_in[k])
        hi, lo = hi * ok_hi, lo * ok_lo
        s_out[k, 0:4, :] = own[k, 0:4, :] + lo[12:16]
        s_out[k, 4:12, :] = own[k, 4:12, :]
        s_out[k, 12:20, :] = own[k, 12:20, :] + hi[0:8]
        s_out[k, 20:28, :] = hi[8:16]
        s_out[k, 28:36, :] = jnp.zeros((8, 128), F32)
        s_out[k, 36:44, :] = lo[0:8]
        s_out[k, 44:48, :] = own[k, 20:24, :] + lo[8:12]
    off_a = jnp.where(px == 0, 5, 0)
    off_b = 5 - off_a
    for out, off in ((a_out, off_a), (b_out, off_b)):
        for k in range(7):
            out[k, 0:28, :] = s_out[off + k, 0:28, :]
            out[k, 28:40, :] = s_out[off + k, 36:48, :]
        for n in range(2):
            hi, lo = hi_lo(py, c_in[12 + n], d_in[12 + n])
            out[7 + n, 0:16, :] = f[16 * n : 16 * n + 16, :]
            out[7 + n, 16:32, :] = hi
            out[9, 16 * n : 16 * n + 16, :] = lo
        out[7, 32:40, :] = jnp.zeros((8, 128), F32)
        out[8, 32:40, :] = jnp.zeros((8, 128), F32)
        out[9, 32:40, :] = jnp.zeros((8, 128), F32)


def down1_shares(info, shares, f, c_in, d_in, a_in, b_in, pairs, packed, f9, s_b1, s_v1, s_b2, s_v2, dom1, dom2, tmp, tmp3):
    ix, iy, px, py = place(info)
    okx_hi, okx_lo = okf(ix < NGX - 1), okf(ix > 0)
    dom1[...] = y_domain(48, 16, 16, iy * 16, W * NGY // 2)
    start1, n1x = ix * 16 - 10, W * NGX // 2
    gap = jnp.zeros((8, 128), F32)

    def wide_y(v):
        return jnp.concatenate([v[0:28], gap, v[28:40]], axis=0)

    for p in range(18):
        total = None
        if 3 <= p < 15:
            total = shares[p - 3]
        if p < 7:
            part = wide_y(hi_lo(px, a_in[p], b_in[p])[1] * okx_lo)
            total = part if total is None else total + part
        if p >= 11:
            part = wide_y(hi_lo(px, a_in[p - 11], b_in[p - 11])[0] * okx_hi)
            total = part if total is None else total + part
        pairs[p] = total * (dom1[...] * x_in(start1, 2 * p, n1x))
    levels_down(info, pairs, s_b1, s_v1, s_b2, s_v2, dom1, dom2, tmp)
    pack3(packed, s_b2, s_v2, tmp, tmp3)
    for n in range(2):
        rows16 = slice(16 * n, 16 * n + 16)
        f9[0, rows16, :] = f[rows16, :]
        hi, lo = hi_lo(py, c_in[12 + n], d_in[12 + n])
        f9[1, rows16, :] = hi
        f9[2, rows16, :] = lo
        hi, lo = hi_lo(px, a_in[7 + n], b_in[7 + n])
        for m in range(2):
            f9[3 + m, rows16, :] = hi[16 * m : 16 * m + 16]
            f9[6 + m, rows16, :] = lo[16 * m : 16 * m + 16]
    hi, lo = hi_lo(px, a_in[9], b_in[9])
    f9[5] = hi[0:32]
    f9[8] = lo[0:32]


def pack1_gx(info, own, c_in, d_in, a_out, b_out):
    ix, iy, px, py = place(info)
    ok_hi, ok_lo = okf(iy < NGY - 1), okf(iy > 0)
    off_a = jnp.where(px == 0, 4, 0)
    off_b = 4 - off_a
    for out, off in ((a_out, off_a), (b_out, off_b)):
        for k in range(4):
            hi, lo = hi_lo(py, c_in[off + k], d_in[off + k])
            out[k, 0:16, :] = own[off + k]
            out[k, 16:24, :] = hi * ok_hi
            out[k, 24:32, :] = lo * ok_lo


def down1(info, own, c_in, d_in, a_in, b_in, pairs, packed, s_b1, s_v1, s_b2, s_v2, dom1, dom2, tmp, tmp3):
    ix, iy, px, py = place(info)
    ok_hi, ok_lo = okf(iy < NGY - 1), okf(iy > 0)
    okx_hi, okx_lo = okf(ix < NGX - 1), okf(ix > 0)
    gap = jnp.zeros((16, 128), F32)
    for k in range(18):
        pairs[k, 24:40, :] = gap
    zero = jnp.zeros((48, 128), F32)
    pairs[0] = zero
    pairs[17] = zero
    for k in range(8):
        hi, lo = hi_lo(py, c_in[k], d_in[k])
        pairs[5 + k, 0:16, :] = own[k]
        pairs[5 + k, 16:24, :] = hi * ok_hi
        pairs[5 + k, 40:48, :] = lo * ok_lo
    for k in range(4):
        hi, lo = hi_lo(px, a_in[k], b_in[k])
        pairs[1 + k, 0:24, :] = lo[0:24] * okx_lo
        pairs[1 + k, 40:48, :] = lo[24:32] * okx_lo
        pairs[13 + k, 0:24, :] = hi[0:24] * okx_hi
        pairs[13 + k, 40:48, :] = hi[24:32] * okx_hi
    levels_down(info, pairs, s_b1, s_v1, s_b2, s_v2, dom1, dom2, tmp)
    pack3(packed, s_b2, s_v2, tmp, tmp3)


def levels_down(info, pairs, b1, v1, b2, v2, dom1, dom2, tmp):
    ix, iy, px, py = place(info)
    n1x, n1y = W * NGX // 2, W * NGY // 2
    dom1[...] = y_domain(48, 16, 16, iy * 16, n1y)
    dom2[...] = y_domain(24, 8, 8, iy * 8, n1y // 2)
    even = (lanes((48, 128)) & 1) == 0
    for k in range(18):
        p = pairs[k]
        b1[2 * k] = jnp.where(even, p, pltpu.roll(p, 1, 1))
        b1[2 * k + 1] = jnp.where(even, pltpu.roll(p, 127, 1), p)
    zero1 = jnp.zeros((48, 128), F32)
    v1[0] = zero1
    v1[35] = zero1
    start1 = ix * 16 - 10
    double_sweep(v1, b1, 1, 35, 2, dom1, start1, n1x)
    start2 = ix * 8 - 4

    def emit2(k, u, r):
        b2[k] = r * dom2[...] * x_in(start2, k, n1x // 2)

    restrict_rows(emit2, v1, b1, tmp, 0, 16, 2, 2, 24)
    zero2 = jnp.zeros((24, 128), F32)
    v2[0] = zero2
    v2[15] = zero2
    double_sweep(v2, b2, 1, 15, 4, dom2, start2, n1x // 2)


def pack3(packed, b2, v2, tmp, tmp3):
    def emit3(k, u, r):
        tmp3[k] = r

    restrict_rows(emit3, v2, b2, tmp, 0, 4, 4, 4, 8)
    row = lax.broadcasted_iota(jnp.int32, (8, 128), 0)
    lane = lanes((8, 128)) & 7
    first = okf((lane == row) & (row < 4))
    second = okf((lane == row + 4) & (row < 4))
    for q in range(2):
        s = tmp3[2 * q] * first + tmp3[2 * q + 1] * second
        tmp3[4 + q, 0:1, :] = jnp.sum(s, axis=0, keepdims=True)
    both = jnp.concatenate([tmp3[4, 0:1, :], tmp3[5, 0:1, :]], axis=0)
    packed[...] = jnp.broadcast_to(both[None], packed.shape)


def again(info, pairs, v0, b1, v1, b2, v2, v_out, dom1, dom2, tmp):
    for i in range(44):
        v_out[i] = v0[i]
    levels_down(info, pairs, b1, v1, b2, v2, dom1, dom2, tmp)


def coarse_up(info, g, pairs, s, ready=None):
    ix, iy, px, py = place(info)
    n3x = NGX * 4

    def load(d, u):
        at = ix - 7 + d
        ok = okf((at >= 0) & (at < NGX))
        at = jnp.clip(at, 0, NGX - 1)
        base = d * 16
        s.px[pl.ds(pl.multiple_of(base, 8), 8), :] = g[at, pl.ds(0, 8, stride=2), :] * ok
        s.px[pl.ds(pl.multiple_of(base + 8, 8), 8), :] = g[at, pl.ds(1, 8, stride=2), :] * ok

    rows(0, 15, 15, load)
    src = lax.broadcasted_iota(jnp.int32, (128, 1024), 0)
    dst = lax.broadcasted_iota(jnp.int32, (128, 1024), 1)
    pick = okf(src == ((dst & 127) >> 3) * 8 + (dst >> 7)).astype(BF16)
    x = s.px[...]
    x_hi, x_lo = split3(x)
    x_lo2 = (x - x_hi.astype(F32) - x_lo.astype(F32)).astype(BF16)
    s.pu[...] = dot(x_hi, pick) + dot(x_lo, pick) + dot(x_lo2, pick)

    def place3(d, u):
        for q in range(2):
            for j in range(8):
                part = s.pu[pl.ds(pl.multiple_of(d * 16 + q * 8, 8), 8), j * 128 : (j + 1) * 128]
                s.b3[d * 4 + 2 * q + (j >> 2), pl.ds(j & 3, 8, stride=4), :] = part

    rows(0, 15, 15, place3)
    e3, e4, e5 = y_edge(32), y_edge(16), y_edge(8)
    start3, start4, start5 = (ix - 7) * 4, (ix - 7) * 2, ix - 7
    z3, z4, z5 = jnp.zeros((32, 128), F32), jnp.zeros((16, 128), F32), jnp.zeros((8, 128), F32)
    for r, z, n in ((s.v3, z3, 60), (s.b4, z4, 30), (s.v4, z4, 30), (s.b5, z5, 15), (s.v5, z5, 15), (s.w5, z5, 15)):
        r[0] = z
        r[n - 1] = z
    double_sweep(s.v3, s.b3, 1, 59, 8, None, start3, n3x, e3)

    def emit4(k, u, r):
        s.b4[k] = r * x_in(start4, k, n3x // 2)

    restrict_rows(emit4, s.v3, s.b3, s.tmp, 1, 29, 0, 8, 16, e3)
    double_sweep(s.v4, s.b4, 1, 29, 16, None, start4, n3x // 2, e4)

    def emit5(k, u, r):
        s.b5[k] = r * x_in(start5, k, NGX)

    restrict_rows(emit5, s.v4, s.b4, s.tmp, 1, 14, 0, 16, 8, e4)
    double_sweep(s.v5, s.b5, 1, 14, 32, None, start5, NGX, e5)
    sweep(s.w5, s.v5, s.b5, 1, 14, 32, None, start5, NGX, e5)
    sweep(s.v5, s.w5, s.b5, 1, 14, 32, None, start5, NGX, e5)

    correct(s.w4, s.v4, s.v5, s.tmp, 5, 10, 0, ((0, 8, 0),), 16, None, start4, n3x // 2)
    sweep(s.v4, s.w4, s.b4, 11, 19, 16, None, start4, n3x // 2, e4)
    correct(s.w3, s.v3, s.v4, s.tmp, 12, 18, 0, ((0, 16, 0),), 32, None, start3, n3x)
    sweep(s.v3, s.w3, s.b3, 26, 34, 8, None, start3, n3x, e3)

    if ready is None:
        levels_down(info, use(pairs), s.b1, s.v1, s.b2, s.v2, s.dom1, s.dom2, s.tmp)
    else:
        s.b1, s.v1, s.b2, s.v2 = [use(r) for r in ready]
        s.dom1[...] = y_domain(48, 16, 16, iy * 16, NGY * 16)
        s.dom2[...] = y_domain(24, 8, 8, iy * 8, NGY * 8)
    turn = lax.rem(32 - 4 * iy, 32)

    def shifted(k):
        return pltpu.roll(s.v3[k + 26], turn, 0)

    start2, start1 = ix * 8 - 4, ix * 16 - 10
    n2x, n1x = n3x * 2, n3x * 4
    correct(s.w2, s.v2, None, s.tmp, 0, 8, 0, ((0, 8, 0), (28, 4, 16)), 24, s.dom2, start2, n2x, shifted)
    sweep(s.e2, s.w2, s.b2, 2, 14, 4, s.dom2, start2, n2x)
    correct(s.w1, s.v1, s.e2, s.tmp, 2, 14, 2, ((0, 24, 0),), 48, s.dom1, start1, n1x)
    sweep(s.e1, s.w1, s.b1, 7, 29, 2, s.dom1, start1, n1x)


class Bag:
    pass


COARSE = (
    ("px", (240, 128)),
    ("pu", (240, 1024)),
    ("b3", (60, 32, 128)),
    ("v3", (60, 32, 128)),
    ("w3", (60, 32, 128)),
    ("b4", (30, 16, 128)),
    ("v4", (30, 16, 128)),
    ("w4", (30, 16, 128)),
    ("b5", (15, 8, 128)),
    ("v5", (15, 8, 128)),
    ("w5", (15, 8, 128)),
    ("w2", (16, 24, 128)),
    ("e2", (16, 24, 128)),
    ("w1", (36, 48, 128)),
    ("e1", (36, 48, 128)),
    ("w0", (44, 48, 128)),
    ("x0", (44, 48, 128)),
    ("dom0", (48, 128)),
    ("dom1", (48, 128)),
    ("dom2", (24, 128)),
    ("b1", (36, 48, 128)),
    ("v1", (36, 48, 128)),
    ("b2", (16, 24, 128)),
    ("v2", (16, 24, 128)),
    ("v0", (44, 48, 128)),
    ("tmp", (32, 48, 128)),
    ("tmp1", (16, 16, 128)),
)
COARSE_SCRATCH = [pltpu.VMEM(shape, F32) for name, shape in COARSE]


OUT_SCRATCH = [pltpu.VMEM((3, W, W, 128), F32), pltpu.VMEM((W, W, 128), F32), pltpu.SemaphoreType.DMA((8,))]


def bag(refs):
    s = Bag()
    for (name, shape), ref in zip(COARSE, refs):
        setattr(s, name, ref)
    return s


PIECES0 = ((0, 20, 0), (44, 4, 40))


def middle(info, g, b0, pairs, v_out, own_out, c_out, d_out, *scratch):
    s = bag(scratch)
    ix, iy, px, py = place(info)
    coarse_up(info, g, pairs, s)
    s.dom0[...] = y_domain(48, W, 8, iy * W, W * NGY)
    start, size = ix * W - 6, W * NGX
    b0 = use(b0)
    zero = jnp.zeros((48, 128), F32)
    s.v0[0] = zero
    s.v0[43] = zero
    double_sweep(s.v0, b0, 1, 43, 1, s.dom0, start, size)
    correct(s.w0, s.v0, s.e1, s.tmp, 7, 29, -14, PIECES0, 48, s.dom0, start, size)
    sweep(s.x0, s.w0, b0, 2, 42, 1, s.dom0, start, size)
    sweep(s.w0, s.x0, b0, 3, 41, 1, s.dom0, start, size)
    sweep(v_out, s.w0, b0, 4, 40, 1, s.dom0, start, size)
    for i in (0, 1, 2, 3, 40, 41, 42, 43):
        v_out[i] = zero
    emit_level1(own_out, c_out, d_out, py, s.tmp1, v_out, b0, s.tmp)


def final(info, g, b0, v0, b1, v1, b2, v2, pushed, vel_out, p_out, vel_buf, p_buf, sems, *scratch):
    s = bag(scratch)
    ix, iy, px, py = place(info)
    coarse_up(info, g, None, s, (b1, v1, b2, v2))
    s.dom0[...] = y_domain(48, W, 8, iy * W, W * NGY)
    start, size = ix * W - 6, W * NGX
    b0, v0 = use(b0), use(v0)
    correct(s.w0, v0, s.e1, s.tmp, 9, 27, -14, PIECES0, 48, s.dom0, start, size)
    sweep(s.x0, s.w0, b0, 5, 39, 1, s.dom0, start, size)
    zm = z_masks(1)
    pushed = use(pushed)
    copies = []
    for t in range(4):
        for x in range(8 * t, 8 * t + 8):
            p = s.x0[x + 6]
            own = p[0:W]
            p_buf[x] = own
            gx = s.x0[x + 7, 0:W, :] - s.x0[x + 5, 0:W, :]
            gy = pltpu.roll(p, 47, 0)[0:W] - pltpu.roll(p, 1, 0)[0:W]
            gz = pltpu.roll(own, 127, 1) * zm[1] - pltpu.roll(own, 1, 1) * zm[0]
            vel_buf[0, x] = pushed[0, x] - 0.5 * gx
            vel_buf[1, x] = pushed[1, x] - 0.5 * gy
            vel_buf[2, x] = pushed[2, x] - 0.5 * gz
        part = pl.ds(8 * t, 8)
        copies.append(pltpu.make_async_copy(vel_buf.at[:, part], vel_out.at[:, part], sems.at[2 * t]))
        copies.append(pltpu.make_async_copy(p_buf.at[part], p_out.at[part], sems.at[2 * t + 1]))
        copies[-2].start()
        copies[-1].start()
    for copy in copies:
        copy.wait()


def push_kernel(info, vel, f9, out):
    ix, iy, px, py = place(info)
    ok = {-1: (okf(ix > 0), okf(iy > 0)), 0: (1.0, 1.0), 1: (okf(ix < NGX - 1), okf(iy < NGY - 1))}
    start_x = (ix * W).astype(F32)
    start_y = (iy * W).astype(F32)
    order = ((0, 0), (0, 1), (0, -1), (1, 0), (1, 1), (1, -1), (-1, 0), (-1, 1), (-1, -1))
    for slot, (ox_, oy_) in enumerate(order):
        q = f9.at[slot]
        cx, cy, cz = vec(q, 6) - start_x, vec(q, 8) - start_y, vec(q, 10)
        ox, oy, oz = vec(q, 12), vec(q, 14), vec(q, 16)
        keep = ok[ox_][0] * ok[oy_][1]
        force = [vec(q, 2 * c) * keep for c in range(3)]
        wx = taps(row_coord(32, 0), cx, ox, tap_norm(ox))
        y0, yn = {0: (0, 32), 1: (24, 8), -1: (0, 8)}[oy_]
        wy = taps(row_coord(yn, y0), cy, oy, tap_norm(oy))
        wz = taps(row_coord(128, 0), cz, oz, tap_norm(oz)).T
        r_hi, r_lo = split3(wz)
        right = jnp.concatenate([r_hi, r_lo, r_hi], axis=0)
        fy = [force[c] * wy for c in range(3)]
        x0, xn = {0: (0, 32), 1: (28, 4), -1: (0, 4)}[ox_]
        step = min(xn, 4 if oy_ == 0 else 16)

        def spread(t, x0=x0, step=step, fy=fy, right=right, y0=y0, yn=yn, slot=slot, wx=wx):
            at = x0 + t * step
            left = []
            for k in range(step):
                row = wx[at + k : at + k + 1, :]
                left += [row * fy[c] for c in range(3)]
            hi, lo = split3(jnp.concatenate(left, axis=0))
            r = dot(jnp.concatenate([hi, hi, lo], axis=1), right).reshape(step, 3, yn, 128)
            for k in range(step):
                for c in range(3):
                    base = vel if slot == 0 else out
                    out[c, at + k, y0 : y0 + yn, :] = base[c, at + k, y0 : y0 + yn, :] + r[k, c]

        for t in range(xn // step):
            spread(t)


def gather3(packed):
    return lax.all_to_all(packed, AXES, 0, 0, tiled=True).reshape(NGX, 16, 128)


LEVELS12 = [(18, 48, 128), (NGX * NGY, 2, 128)]
DOWN1 = [
    VMEM((36, 48, 128), F32), VMEM((36, 48, 128), F32), VMEM((16, 24, 128), F32), VMEM((16, 24, 128), F32),
    VMEM((48, 128), F32), VMEM((24, 128), F32), VMEM((32, 48, 128), F32), VMEM((6, 8, 128), F32),
]


def per_device(velocity, point_cells, point_offsets, point_count, drag, blade_speed):
    info = jnp.stack([lax.axis_index("gx"), lax.axis_index("gy"), point_count.reshape(())]).astype(jnp.int32)

    py = lax.axis_index("gy") % 2
    top, bottom = velocity[:, :, W - 4 :, :].reshape(3 * W, 4, 128), velocity[:, :, :4, :].reshape(3 * W, 4, 128)
    c0, d0 = swap_gy(jnp.where(py == 0, top, bottom), jnp.where(py == 0, bottom, top))
    a0, b0 = call(pack_gx, [(12, 40, 128)] * 2, [], info, velocity[:, :4], velocity[:, W - 4 :], c0, d0)
    a0, b0 = swap_gx(a0, b0)
    part, xt, yt, zt, rv = call(
        sample_kernel, [(3, 40, P_), (2, 48, P_), (2, 48, P_), (2, P_, 128), (W, W, 128)], [], info, velocity, point_cells, point_offsets, c0, d0
    )
    g, f, own1, c1, d1 = call(
        force_kernel,
        [(50, 48, 128), (32, 128), (12, 24, 128), (14, 16, 128), (14, 16, 128)],
        [
            VMEM((50, 48, 128), F32), VMEM((48, 128), F32),
            VMEM((32, 48, 128), F32), VMEM((24, 24, 128), F32),
        ],
        info, point_cells, point_offsets, drag, blade_speed, part, xt, yt, zt, rv, a0, b0,
    )
    c1, d1 = swap_gy(c1, d1)
    shares, a1, b1 = call(merge1_gx, [(12, 48, 128), (10, 40, 128), (10, 40, 128)], [], info, own1, f, c1, d1)
    a1, b1 = swap_gx(a1, b1)
    pairs, packed, f9 = call(down1_shares, LEVELS12 + [(9, 32, 128)], DOWN1, info, shares, f, c1, d1, a1, b1)
    cg, dg = call(pack_g, [(42, 16, 128)] * 2, [], info, g)
    packed, g, cg, dg, f9 = lax.optimization_barrier((packed, g, cg, dg, f9))
    gathered = gather3(packed)
    cg, dg = swap_gy(cg, dg)
    h, ag, bg = call(merge_g, [(42, 48, 128), (11, 48, 128), (11, 48, 128)], [], info, g, cg, dg)
    ag, bg = swap_gx(ag, bg)
    (rhs,) = call(down0, [(44, 48, 128)], [VMEM((48, 128), F32)], info, h, ag, bg)
    v0, own1, c1, d1 = call(
        middle, [(44, 48, 128), (8, 16, 128), (8, 8, 128), (8, 8, 128)], COARSE_SCRATCH, info, gathered, rhs, pairs
    )
    c1, d1 = swap_gy(c1, d1)
    a1, b1 = call(pack1_gx, [(4, 32, 128)] * 2, [], info, own1, c1, d1)
    a1, b1 = swap_gx(a1, b1)
    pairs, packed = call(down1, LEVELS12, DOWN1, info, own1, c1, d1, a1, b1)
    packed, pairs, v0 = lax.optimization_barrier((packed, pairs, v0))
    gathered = gather3(packed)
    *levels, v0 = call(
        again, [(36, 48, 128), (36, 48, 128), (16, 24, 128), (16, 24, 128), (44, 48, 128)],
        [VMEM((48, 128), F32), VMEM((24, 128), F32), VMEM((32, 48, 128), F32)], info, pairs, v0,
    )
    (pushed,) = call(push_kernel, [(3, W, W, 128)], [], info, velocity, f9)
    vel_out, p_out = call(
        final, [(3, W, W, 128), (W, W, 128)], OUT_SCRATCH + COARSE_SCRATCH, info, gathered, rhs, v0, *levels, pushed,
        late=(2, 3, 4, 5, 6, 7, 8), direct=(0, 1),
    )
    return vel_out, p_out


def solution(mesh):
    placed = (
        P(None, "gx", "gy", None),
        P(None, "gx", "gy", None),
        P(None, "gx", "gy", None),
        P("gx", "gy"),
        P("gx", "gy", None),
        P("gx", "gy", None),
    )
    return jax.shard_map(
        per_device,
        mesh=mesh,
        in_specs=placed,
        out_specs=(P(None, "gx", "gy", None), P("gx", "gy", None)),
        check_vma=False,
    )
```
